256 devices in a mesh: blk: 8 (over y, x_lo), cross: 32 (over x_hi, z, core).
Axes of the slice: x: 4 (x_hi: 2, x_lo: 2; x = x_hi * 2 + x_lo), y: 4, z: 8, core: 2. Of those that a mesh axis runs over, the one named last changes fastest.
Arguments:
- right_side: float32 [16, 32, 512, 256], P('blk', 'cross'), may hold values from -6 to 6
- schur_inverse: bfloat16 [16, 32, 1024, 1024], P('blk', 'cross'), may hold values from -1 to 3, as said below
- schur: bfloat16 [16, 32, 1024, 1024], P('blk', 'cross'), may hold values from -1 to 3, as said below
- coarse_basis: float32 [16, 32, 4, 512], P('blk', 'cross'), may hold values from -1.25 to 1.25
- occupancy: int32 [16, 32, 512], P('blk', 'cross'), may hold values 0 or 1
- perm_left: int32 [16, 32, 256], P('blk', 'cross'), may hold values from 0 to 255, each once within a row
- perm_down: int32 [16, 32, 256], P('blk', 'cross'), may hold values from 0 to 255, each once within a row
- corner_number: int32 [512], replicated, may hold values from 0 to 511, each once
- coarse_inverse: float32 [512, 512], replicated, may hold values from -1 to 3, as said below
Outputs:
- multipliers: float32 [16, 32, 512, 256], P('blk', 'cross')
The draws below stay inside these ranges and needn't reach their ends.
Inputs may be any that keep to these rules, and one draw needn't show every extreme that they name: `perm_left`: each row holds every number 0 to 255 once. `perm_down`: each row holds every number 0 to 255 once. `corner_number`: holds every number 0 to 511 once. `schur_inverse`: every block is symmetric positive definite. `schur`: every block is symmetric positive definite. `coarse_inverse`: symmetric positive definite.
All inputs are finite; a program needn't handle non-finite values. No bound on the sum of `occupancy` on one device may be relied on, other than what follows from the above.
Results may differ from the reference program's by a relative error of at most 0.0023.
The reference program's roundings to bfloat16 on the way (of `operand`) count: a program that leaves them out, or rounds other values in their place, can miss the bound.
Values sent between devices are 32-bit elements; how exact they have to be, the bound alone decides.
No kernel may reach another device: no remote copies, remote signals or barrier semaphores. Data moves between devices by JAX's collectives and lax.ppermute only.
A program may use at most 64 MiB of HBM per device.

```python
import jax
import jax.numpy as jnp
from jax import lax

M = 1024
FACE = 256
MULT = 512
RHS = 256
ITERS = 2
CORNERS = 4
NA = 16
NS = 32
NC = 512


def spd_block(key, order):
    noise_key, diag_key = jax.random.split(key)
    noise = jax.random.uniform(noise_key, (order, order), jnp.float32, -1.0, 1.0)
    mixed = (noise + jnp.transpose(noise)) * (0.37 / order ** 0.5)
    diagonal = jax.random.uniform(diag_key, (order,), jnp.float32, 1.0, 2.0)
    rows = lax.broadcasted_iota(jnp.int32, (order, order), 0)
    columns = lax.broadcasted_iota(jnp.int32, (order, order), 1)
    return jnp.where(rows == columns, diagonal[:, None], mixed)


def spd_stack(key, count, order):

    def one_block(position):
        return spd_block(jax.random.fold_in(key, position), order).astype(jnp.bfloat16)
    return lax.map(one_block, jnp.arange(count, dtype=jnp.int32))


def draw_schur_inverse(key, part):
    stack = spd_stack(jax.random.fold_in(key, 11), NA * NS, M)
    return stack.reshape(NA, NS, M, M)


def draw_schur(key, part):
    stack = spd_stack(jax.random.fold_in(key, 23), NA * NS, M)
    return stack.reshape(NA, NS, M, M)


def draw_coarse_inverse(key, part):
    return spd_block(jax.random.fold_in(key, 37), NC)


def set_ends(values, rng, least, largest):
    dims = values.shape
    index_at = [jax.random.randint(jax.random.fold_in(rng, axis), (), 0, dims[axis]) for axis in range(len(dims))]
    values = values.at[tuple(index_at)].set(least)
    longest = dims.index(max(dims))
    index_at[longest] = (index_at[longest] + 1) % dims[longest]
    return values.at[tuple(index_at)].set(largest)


def block_levels(stream_key, extent, cuts, smallest, largest):
    def one(dim, parts):
        draws = jax.random.uniform(jax.random.fold_in(jax.random.fold_in(stream_key, 6), dim), (parts,), jnp.float32, smallest / len(cuts), largest / len(cuts))
        return jnp.repeat(jnp.exp(draws), extent[dim] // parts).reshape((-1,) + (1,) * (len(extent) - dim - 1))

    level = one(*cuts[0])
    for cut in cuts[1:]:
        level = level * one(*cut)
    return level


def centred(stream_key, shape, scale, bound, pieces=(), held_as=jnp.bfloat16):
    values = scale * jax.random.normal(stream_key, shape, jnp.float32)
    if pieces:
        values = values * block_levels(stream_key, shape, pieces, -0.22, 0.18)
    return jnp.clip(values, -bound, bound).astype(held_as)


def setup_inputs(seed: int = 0) -> dict:
    arg_keys = jax.random.split(jax.random.key(seed), 10)
    return {
        "right_side": centred(arg_keys[0], (NA, NS, MULT, RHS), 1.0, 6.0, ((0, 8), (1, 32)), jnp.float32),
        "schur_inverse": draw_schur_inverse(jax.random.fold_in(arg_keys[9], 71), 0),
        "schur": draw_schur(jax.random.fold_in(arg_keys[9], 71), 0),
        "coarse_basis": centred(arg_keys[3], (NA, NS, CORNERS, MULT), (2.0 / MULT ** 0.5), 1.25, ((0, 8), (1, 32)), jnp.float32),
        "occupancy": set_ends((jax.random.randint(arg_keys[4], (NA, NS, MULT), 0, 2) < 1).astype(jnp.int32), jax.random.fold_in(arg_keys[4], 1), 0, 1),
        "perm_left": jax.vmap(lambda own: jax.random.permutation(own, FACE))(jax.random.split(arg_keys[5], NA * NS)).reshape((NA, NS, FACE)).astype(jnp.int32),
        "perm_down": jax.vmap(lambda own: jax.random.permutation(own, FACE))(jax.random.split(arg_keys[6], NA * NS)).reshape((NA, NS, FACE)).astype(jnp.int32),
        "corner_number": jax.random.permutation(arg_keys[7], NC).astype(jnp.int32),
        "coarse_inverse": draw_coarse_inverse(jax.random.fold_in(arg_keys[9], 71), 0),
    }


exact_mode = lax.Precision.HIGHEST


def rows_by(face, order):
    lead = face.shape[:2]
    flat = face.reshape((-1,) + face.shape[2:])
    picks = order.reshape((-1, order.shape[-1]))
    taken = jax.vmap(lambda block, chosen: jnp.take(block, chosen, axis=0))(flat, picks)
    return taken.reshape(lead + taken.shape[1:])


def spread(multiplier, left_order, down_order):
    faces = multiplier.shape[2] // 2
    right = multiplier[:, :, :faces]
    upper = multiplier[:, :, faces:]
    left = -rows_by(jnp.roll(right, 1, axis=1), left_order)
    down = -rows_by(jnp.roll(upper, 1, axis=0), down_order)
    return jnp.concatenate([left, right, down, upper], axis=2)


def jump(image, left_inverse, down_inverse):
    faces = image.shape[2] // 4
    left = rows_by(image[:, :, :faces], left_inverse)
    down = rows_by(image[:, :, 2 * faces:3 * faces], down_inverse)
    right = image[:, :, faces:2 * faces] - jnp.roll(left, -1, axis=1)
    upper = image[:, :, 3 * faces:] - jnp.roll(down, -1, axis=0)
    return jnp.concatenate([right, upper], axis=2)


def apply_blocks(matrices, operand):
    lead = operand.shape[:2]
    flat_mats = matrices.reshape((-1,) + matrices.shape[2:])
    flat_operand = operand.reshape((-1,) + operand.shape[2:])
    result = lax.map(lambda pair: jnp.dot(pair[0], pair[1], preferred_element_type=jnp.float32), (flat_mats, flat_operand))
    return result.reshape(lead + result.shape[1:])


def reference(right_side, schur_inverse, schur, coarse_basis, occupancy, perm_left, perm_down, corner_number, coarse_inverse):
    axial_count = right_side.shape[0]
    sector_count = right_side.shape[1]
    corner_count = coarse_inverse.shape[0]
    weight = 1.0 / (1.0 + occupancy.astype(jnp.float32))
    left_inverse = jnp.argsort(perm_left, axis=-1).astype(jnp.int32)
    down_inverse = jnp.argsort(perm_down, axis=-1).astype(jnp.int32)
    numbers = corner_number.reshape(axial_count, sector_count)
    corner_ids = jnp.stack([numbers, jnp.roll(numbers, -1, axis=1), jnp.roll(numbers, -1, axis=0), jnp.roll(numbers, (-1, -1), axis=(0, 1))], axis=2)

    def precondition(residual):
        weighted = weight[..., None] * residual
        operand = spread(weighted, perm_left, perm_down).astype(jnp.bfloat16)
        image = apply_blocks(schur, operand)
        local = weight[..., None] * jump(image, left_inverse, down_inverse)
        loads = jnp.einsum("abcm,abmr->abcr", coarse_basis, residual, precision=exact_mode)
        corner_sums = jax.ops.segment_sum(loads.reshape(-1, loads.shape[-1]), corner_ids.reshape(-1), num_segments=corner_count)
        corner_values = jnp.dot(coarse_inverse, corner_sums, precision=exact_mode, preferred_element_type=jnp.float32)
        return local + jnp.einsum("abcm,abcr->abmr", coarse_basis, corner_values[corner_ids], precision=exact_mode)

    def operate(direction):
        operand = spread(direction, perm_left, perm_down).astype(jnp.bfloat16)
        return jump(apply_blocks(schur_inverse, operand), left_inverse, down_inverse)

    multipliers = jnp.zeros_like(right_side)
    residual = right_side
    smoothed = precondition(residual)
    direction = smoothed
    progress_now = jnp.sum(residual * smoothed, axis=(0, 1, 2))
    for step in range(ITERS):
        image = operate(direction)
        alpha = progress_now / jnp.sum(direction * image, axis=(0, 1, 2))
        multipliers = multipliers + alpha * direction
        if step + 1 < ITERS:
            residual = residual - alpha * image
            smoothed = precondition(residual)
            progress_next = jnp.sum(residual * smoothed, axis=(0, 1, 2))
            direction = smoothed + (progress_next / progress_now) * direction
            progress_now = progress_next
    return multipliers
```

```python
import functools

import jax
import jax.numpy as jnp
import numpy as np
from jax import lax
from jax.experimental import pallas as pl
from jax.experimental.pallas import tpu as pltpu
from jax.sharding import Mesh
from jax.sharding import PartitionSpec as P

SPLIT = {"y": 4, "xl": 2, "xh": 2, "z": 8, "c": 2}
BLK = ("y", "xl")
CROSS = ("xh", "z", "c")
NEAR = ("z", "c")
FAR = ("y", "xl", "xh")
F = 256
R = 256
CORNERS = 512
EXACT = lax.Precision.HIGHEST
F32 = jnp.float32
BF16 = jnp.bfloat16

FACES = 7
SIDES = ((4, 0, 6, 2), (5, 1, 2, 3))
OWNER = ((0, 0), (1, 0), (0, 0), (1, 0), (0, -1), (1, -1), (-1, 0))


def slot(axial, sector):
    return (axial + 1) * 3 + sector + 1


SLOTS = 16


def face_slots(face):
    axial, sector = OWNER[face]
    return [slot(axial + da, sector + ds) for da in (0, 1) for ds in (0, 1)]


def call(kernel, outs, *args, flops=0, smem=()):
    size = sum(int(np.prod(a.shape)) * a.dtype.itemsize for a in args)
    size += sum(int(np.prod(s)) * jnp.dtype(d).itemsize for s, d in outs)
    return pl.pallas_call(
        kernel,
        out_shape=[jax.ShapeDtypeStruct(s, d) for s, d in outs],
        in_specs=[
            pl.BlockSpec(memory_space=pltpu.SMEM if i in smem else pltpu.VMEM)
            for i in range(len(args))
        ],
        out_specs=[pl.BlockSpec(memory_space=pltpu.VMEM)] * len(outs),
        compiler_params=pltpu.CompilerParams(vmem_limit_bytes=40 * 1024 * 1024),
        cost_estimate=pl.CostEstimate(flops=flops, bytes_accessed=size, transcendentals=0),
    )(*args)


def thirds(value):
    high = value.astype(BF16)
    rest = value - high.astype(F32)
    middle = rest.astype(BF16)
    return high, middle, (rest - middle.astype(F32)).astype(BF16)


def nt(left, right):
    return lax.dot_general(left, right, (((1,), (1,)), ((), ())), preferred_element_type=F32)


def tn(left, right):
    return lax.dot_general(left, right, (((0,), (0,)), ((), ())), preferred_element_type=F32)


def nn(left, right):
    return lax.dot_general(left, right, (((1,), (0,)), ((), ())), preferred_element_type=F32)


def pack_kernel(r_ref, occ_ref, basis_ref, right_ref, up_ref, small_right_ref, small_up_ref):
    for k in range(2):
        right_ref[k] = r_ref[k, :F, :]
    up_ref[...] = r_ref[1, F:, :]
    weight = 1.0 / (1.0 + occ_ref[...].astype(F32))
    small_right_ref[...] = jnp.zeros_like(small_right_ref)
    small_up_ref[...] = jnp.zeros_like(small_up_ref)
    for k in range(2):
        small_right_ref[k, 0:4, :] = basis_ref[k, :, :F]
        small_right_ref[k, 4:5, :] = weight[k : k + 1, :F]
    small_up_ref[0:4, :] = basis_ref[1, :, F:]
    small_up_ref[4:5, :] = weight[1:2, F:]


def loads_kernel(r_ref, basis_ref, out_ref):
    out_ref[...] = jnp.zeros_like(out_ref)
    first = jnp.dot(basis_ref[0], r_ref[0], precision=EXACT, preferred_element_type=F32)
    second = jnp.dot(basis_ref[1], r_ref[1], precision=EXACT, preferred_element_type=F32)
    here = slot(0, 0)
    out_ref[here : here + 2, :] = first[0:2]
    here = slot(1, 0)
    out_ref[here : here + 2, :] = first[2:4] + second[0:2]
    here = slot(2, 0)
    out_ref[here : here + 2, :] = second[2:4]


def placed(order_row, scale_row):
    rows = lax.broadcasted_iota(jnp.int32, (F, F), 0)
    onehot = order_row == rows
    if scale_row is None:
        return jnp.where(onehot, -1.0, 0.0).astype(BF16)
    eye = lax.broadcasted_iota(jnp.int32, (F, F), 1) == rows
    column = jnp.sum(jnp.where(eye, scale_row, 0.0), axis=1, keepdims=True)
    return jnp.where(onehot, -column, 0.0).astype(BF16)


def scale_column(row):
    eye = lax.broadcasted_iota(jnp.int32, (F, F), 1) == lax.broadcasted_iota(jnp.int32, (F, F), 0)
    return jnp.sum(jnp.where(eye, row, 0.0), axis=1, keepdims=True)


def reorder_block(s_ref, out_ref, work_ref, k, left_t, down_t, rows_weights):
    work_ref[:, 0:F] = nt(s_ref[k, :, 0:F], left_t).astype(BF16)
    work_ref[:, 2 * F : 3 * F] = nt(s_ref[k, :, 2 * F : 3 * F], down_t).astype(BF16)
    for side in (1, 3):
        part = s_ref[k, :, side * F : (side + 1) * F]
        if rows_weights is not None:
            part = (part.astype(F32) * rows_weights[side]).astype(BF16)
        work_ref[:, side * F : (side + 1) * F] = part
    out_ref[k, 0:F, :] = nn(left_t, work_ref[0:F, :]).astype(BF16)
    out_ref[k, 2 * F : 3 * F, :] = nn(down_t, work_ref[2 * F : 3 * F, :]).astype(BF16)
    for side in (1, 3):
        part = work_ref[side * F : (side + 1) * F, :]
        if rows_weights is not None:
            part = (part.astype(F32) * scale_column(rows_weights[side])).astype(BF16)
        out_ref[k, side * F : (side + 1) * F, :] = part


def reorder_plain_kernel(s_ref, left_ref, down_ref, out_ref):
    def run(work_ref):
        for k in range(2):
            left_t = placed(left_ref[k : k + 1, :], None)
            down_t = placed(down_ref[k : k + 1, :], None)
            reorder_block(s_ref, out_ref, work_ref, k, left_t, down_t, None)

    pl.run_scoped(run, pltpu.VMEM((4 * F, 4 * F), BF16))


def reorder_weighted_kernel(
    s_ref, left_ref, down_ref, occ_ref, basis_ref, from_left_ref, from_down_ref, out_ref, spread_basis_ref
):
    weight = 1.0 / (1.0 + occ_ref[...].astype(F32))
    down_weight = (from_down_ref[4:5, :], weight[0:1, F:])

    def run(work_ref):
        for k in range(2):
            left_t = placed(left_ref[k : k + 1, :], from_left_ref[k, 4:5, :])
            down_t = placed(down_ref[k : k + 1, :], down_weight[k])
            rows = {1: weight[k : k + 1, :F], 3: weight[k : k + 1, F:]}
            reorder_block(s_ref, out_ref, work_ref, k, left_t, down_t, rows)

    pl.run_scoped(run, pltpu.VMEM((4 * F, 4 * F), BF16))
    spread_basis_ref[...] = jnp.zeros_like(spread_basis_ref)
    sources = (
        basis_ref[0, :, :F],
        basis_ref[1, :, :F],
        basis_ref[0, :, F:],
        basis_ref[1, :, F:],
        from_left_ref[0, 0:4, :],
        from_left_ref[1, 0:4, :],
        from_down_ref[0:4, :],
    )
    for face in range(FACES):
        for k, row in enumerate(face_slots(face)):
            spread_basis_ref[face, row : row + 1, :] = sources[face][k : k + 1, :]


def corner_onehot(numbers_t, axial, sector, spare):
    wanted = (axial & 15) * 32 + (sector & 31)
    columns = lax.broadcasted_iota(jnp.int32, (wanted.shape[0], CORNERS), 1)
    picks = jnp.where((columns == wanted) & jnp.logical_not(spare), 1.0, 0.0).astype(BF16)
    return nt(picks, numbers_t).astype(BF16)


def coarse_block_kernel(place_ref, numbers_ref, inverse_ref, out_ref):
    blk, xh, near = place_ref[0], place_ref[1], place_ref[2]
    ids = lax.broadcasted_iota(jnp.int32, (CORNERS, CORNERS), 0)
    numbers_t = jnp.where(numbers_ref[...] == ids, 1.0, 0.0).astype(BF16)
    rows = lax.broadcasted_iota(jnp.int32, (16 * SLOTS, 1), 0)
    peer = rows >> 4
    entry = rows & 15
    third = (entry >= 3).astype(jnp.int32) + (entry >= 6).astype(jnp.int32) + (entry >= 9).astype(jnp.int32)
    da = third - 1
    ds = entry - 3 * third - 1
    spare = entry >= 12
    far_rows = corner_onehot(numbers_t, 2 * (peer >> 1) + da, (peer & 1) * 16 + near + ds, spare)
    near_rows = corner_onehot(numbers_t, 2 * blk + da, xh * 16 + peer + ds, spare)
    picked = sum(nn(far_rows, part) for part in thirds(inverse_ref[...])[::-1])
    block = sum(nt(part, near_rows) for part in thirds(picked)[::-1])
    columns = lax.broadcasted_iota(jnp.int32, (16 * SLOTS, 16 * SLOTS), 1) & 15
    passed = (columns == entry) & spare
    out_ref[...] = jnp.where(passed, 1.0, block)


HALVES = [((2, F, R), F32), ((2, F, R), F32), ((F, R), F32), ((F, R), F32), ((F, R), F32)]


def apply_block(s_ref, operand_ref, left_ref, right_ref, up_ref, down_ref, mid_ref):
    for k in range(2):
        sides = [nn(s_ref[k, side * F : (side + 1) * F, :], operand_ref[k]) for side in range(4)]
        left_ref[k] = sides[0]
        right_ref[k] = sides[1]
        if k == 0:
            down_ref[...] = sides[2]
            mid_ref[...] = sides[3]
        else:
            mid_ref[...] += sides[2]
            up_ref[...] = sides[3]


def set_operand(operand_ref, face, value):
    value = value.astype(BF16)
    for k in range(2):
        for side in range(4):
            if SIDES[k][side] == face:
                operand_ref[k, side * F : (side + 1) * F, :] = value


def first_kernel(s_ref, r_ref, from_left_ref, from_down_ref, left_ref, right_ref, up_ref, down_ref, mid_ref):
    def run(operand_ref):
        for k in range(2):
            set_operand(operand_ref, k, r_ref[k, :F, :])
            set_operand(operand_ref, 2 + k, r_ref[k, F:, :])
            set_operand(operand_ref, 4 + k, from_left_ref[k])
        set_operand(operand_ref, 6, from_down_ref[...])
        apply_block(s_ref, operand_ref, left_ref, right_ref, up_ref, down_ref, mid_ref)

    pl.run_scoped(run, pltpu.VMEM((2, 4 * F, R), BF16))


def faces_of(left_ref, right_ref, up_ref, down_ref, mid_ref):
    return (
        right_ref.at[0],
        right_ref.at[1],
        mid_ref,
        up_ref,
        left_ref.at[0],
        left_ref.at[1],
        down_ref,
    )


def others_of(from_left_ref, from_right_ref, from_up_ref, from_down_ref):
    return (
        from_right_ref.at[0],
        from_right_ref.at[1],
        None,
        from_up_ref,
        from_left_ref.at[0],
        from_left_ref.at[1],
        from_down_ref,
    )


def corner_part(spread_basis_ref, face, values):
    return lax.dot_general(
        spread_basis_ref[face], values, (((0,), (0,)), ((), ())), precision=EXACT, preferred_element_type=F32
    )


def own_face(r_ref, face):
    return r_ref[face % 2, (face // 2) * F : (face // 2 + 1) * F, :]


def total(value):
    return jnp.sum(value, axis=0, keepdims=True)


def operate_first_kernel(
    s_ref, basis_ref, r_ref, values_ref, l_ref, r2_ref, u_ref, d_ref, m_ref, fl_ref, fr_ref, fu_ref, fd_ref,
    z_ref, left_ref, right_ref, up_ref, down_ref, mid_ref, message_ref, corners_ref,
):
    corners = jnp.sum(values_ref[...], axis=0)
    corners_ref[...] = corners
    mine = faces_of(l_ref, r2_ref, u_ref, d_ref, m_ref)
    theirs = others_of(fl_ref, fr_ref, fu_ref, fd_ref)

    def run(operand_ref):
        progress = jnp.zeros((1, R), F32)
        for face in range(FACES):
            value = mine[face][...]
            if theirs[face] is not None:
                value = value + theirs[face][...]
            value = value + corner_part(basis_ref, face, corners)
            z_ref[face] = value
            set_operand(operand_ref, face, value)
            if face < 4:
                progress = progress + total(own_face(r_ref, face) * value)
        apply_block(s_ref, operand_ref, left_ref, right_ref, up_ref, down_ref, mid_ref)
        images = faces_of(left_ref, right_ref, up_ref, down_ref, mid_ref)
        loads = jnp.zeros((SLOTS, R), F32)
        curvature = jnp.zeros((1, R), F32)
        for face in range(FACES):
            image = images[face][...]
            loads = loads + jnp.dot(basis_ref[face], image, precision=EXACT, preferred_element_type=F32)
            curvature = curvature + total(z_ref[face] * image)
        message_ref[...] = loads
        message_ref[12:13, :] = progress
        message_ref[13:14, :] = curvature

    pl.run_scoped(run, pltpu.VMEM((2, 4 * F, R), BF16))


def second_kernel(
    s_ref, r_ref, r_left_ref, r_down_ref, values_ref, corners_ref,
    l_ref, r2_ref, u_ref, d_ref, m_ref, fl_ref, fr_ref, fu_ref, fd_ref,
    residual_ref, image_ref, left_ref, right_ref, up_ref, down_ref, mid_ref, next_ref, scalars_ref,
):
    sums = jnp.sum(values_ref[...], axis=0)
    progress, curvature = sums[12:13, :], sums[13:14, :]
    alpha = progress / curvature
    next_ref[...] = corners_ref[...] - alpha * sums
    scalars_ref[...] = jnp.zeros_like(scalars_ref)
    scalars_ref[0:1, :] = progress
    scalars_ref[1:2, :] = curvature
    scalars_ref[2:3, :] = alpha
    mine = faces_of(l_ref, r2_ref, u_ref, d_ref, m_ref)
    theirs = others_of(fl_ref, fr_ref, fu_ref, fd_ref)

    def run(operand_ref):
        for face in range(FACES):
            image = mine[face][...]
            if theirs[face] is not None:
                image = image + theirs[face][...]
            if face < 4:
                start = own_face(r_ref, face)
            elif face < 6:
                start = r_left_ref[face - 4]
            else:
                start = r_down_ref[...]
            value = start - alpha * image
            if face < 4:
                image_ref[face] = image
                residual_ref[face] = value
            set_operand(operand_ref, face, value)
        apply_block(s_ref, operand_ref, left_ref, right_ref, up_ref, down_ref, mid_ref)

    pl.run_scoped(run, pltpu.VMEM((2, 4 * F, R), BF16))


def operate_last_kernel(
    s_ref, basis_ref, corners_ref, z0_ref, residual_ref, image_ref,
    l_ref, r2_ref, u_ref, d_ref, m_ref, fl_ref, fr_ref, fu_ref, fd_ref,
    z_ref, message_ref,
):
    corners = corners_ref[...]
    rows = lax.broadcasted_iota(jnp.int32, corners.shape, 0)
    corners = jnp.where(rows < 12, corners, 0.0)
    mine = faces_of(l_ref, r2_ref, u_ref, d_ref, m_ref)
    theirs = others_of(fl_ref, fr_ref, fu_ref, fd_ref)

    def run(operand_ref, z7_ref, left_ref, right_ref, up_ref, down_ref, mid_ref):
        progress = jnp.zeros((1, R), F32)
        mixed = jnp.zeros((1, R), F32)
        for face in range(FACES):
            value = mine[face][...]
            if theirs[face] is not None:
                value = value + theirs[face][...]
            value = value + corner_part(basis_ref, face, corners)
            z7_ref[face] = value
            set_operand(operand_ref, face, value)
            if face < 4:
                z_ref[face] = value
                progress = progress + total(residual_ref[face] * value)
                mixed = mixed + total(image_ref[face] * value)
        apply_block(s_ref, operand_ref, left_ref, right_ref, up_ref, down_ref, mid_ref)
        images = faces_of(left_ref, right_ref, up_ref, down_ref, mid_ref)
        curvature = jnp.zeros((1, R), F32)
        for face in range(FACES):
            image = images[face][...]
            curvature = curvature + total(z7_ref[face] * image)
            mixed = mixed + total(z0_ref[face] * image)
        message_ref[...] = jnp.zeros_like(message_ref)
        message_ref[0:1, :] = progress
        message_ref[1:2, :] = curvature
        message_ref[2:3, :] = mixed

    pl.run_scoped(
        run,
        pltpu.VMEM((2, 4 * F, R), BF16),
        pltpu.VMEM((FACES, F, R), F32),
        *[pltpu.VMEM(s, d) for s, d in HALVES],
    )


def finish_kernel(z0_ref, z1_ref, scalars_ref, sums_ref, out_ref):
    sums = jnp.sum(sums_ref[...], axis=0)
    progress, curvature, mixed = sums[0:1, :], sums[1:2, :], sums[2:3, :]
    first_progress, first_curvature, alpha = scalars_ref[0:1, :], scalars_ref[1:2, :], scalars_ref[2:3, :]
    ratio = progress / first_progress
    last = progress / (curvature + ratio * (mixed + ratio * first_curvature))
    scale0 = alpha + last * ratio
    for face in range(4):
        out_ref[face % 2, (face // 2) * F : (face // 2 + 1) * F, :] = scale0 * z0_ref[face] + last * z1_ref[face]


def partial_kernel(block_ref, message_ref, out_ref):
    flat = jnp.concatenate([message_ref[i] for i in range(16)], axis=0)
    out = jnp.dot(block_ref[...], flat, precision=EXACT, preferred_element_type=F32)
    for i in range(16):
        out_ref[i] = out[i * SLOTS : (i + 1) * SLOTS]


def sum_kernel(in_ref, out_ref):
    total_rows = jnp.sum(in_ref[...], axis=0)
    for i in range(16):
        out_ref[i] = total_rows


def moved(block, axes, count, distance):
    return lax.ppermute(block, axes, [(i, (i + distance) % count) for i in range(count)])


def exchanged(left, right, up, down):
    return (
        moved(right, CROSS, 32, 1),
        moved(left, CROSS, 32, -1),
        moved(down, BLK, 8, -1),
        moved(up, BLK, 8, 1),
    )


MATMUL_FLOPS = 2 * 2 * (4 * F) * (4 * F) * R


def on_device(r, s_inverse, s, basis, occ, left_order, down_order, numbers, coarse_inverse):
    r, s_inverse, s = r[:, 0], s_inverse[:, 0], s[:, 0]
    basis, occ, left_order, down_order = basis[:, 0], occ[:, 0], left_order[:, 0], down_order[:, 0]
    place = jnp.stack([lax.axis_index(BLK), lax.axis_index("xh"), lax.axis_index(NEAR)]).astype(jnp.int32)

    right, up, small_right, small_up = call(
        pack_kernel,
        [((2, F, R), F32), ((F, R), F32), ((2, 8, F), F32), ((8, F), F32)],
        r, occ, basis,
    )
    small_left = moved(small_right, CROSS, 32, 1)
    small_down = moved(small_up, BLK, 8, 1)
    r_left = moved(right, CROSS, 32, 1)
    r_down = moved(up, BLK, 8, 1)
    (loads,) = call(loads_kernel, [((SLOTS, R), F32)], r, basis)
    (inverse_block,) = call(
        reorder_plain_kernel, [(s_inverse.shape, BF16)], s_inverse, left_order, down_order, flops=2 * MATMUL_FLOPS
    )
    (coarse_block,) = call(
        coarse_block_kernel,
        [((16 * SLOTS, 16 * SLOTS), F32)],
        place, numbers[None, :], coarse_inverse,
        smem=(0,),
    )

    def coarse(message):
        near = lax.all_gather(message, NEAR)
        (partial,) = call(partial_kernel, [((16, SLOTS, R), F32)], coarse_block, near)
        return lax.all_to_all(partial, FAR, 0, 0)

    schur_block, spread_basis = call(
        reorder_weighted_kernel,
        [(s.shape, BF16), ((FACES, SLOTS, F), F32)],
        s, left_order, down_order, occ, basis, small_left, small_down,
        flops=2 * MATMUL_FLOPS,
    )
    values = coarse(loads)

    halves = call(first_kernel, HALVES, schur_block, r, r_left, r_down, flops=MATMUL_FLOPS)
    others = exchanged(*halves[:4])
    z0, *halves, message, corners = call(
        operate_first_kernel,
        [((FACES, F, R), F32), *HALVES, ((SLOTS, R), F32), ((SLOTS, R), F32)],
        inverse_block, spread_basis, r, values, *halves, *others,
        flops=MATMUL_FLOPS,
    )
    others = exchanged(*halves[:4])
    values = coarse(message)
    residual, image, *halves, corners, scalars = call(
        second_kernel,
        [((4, F, R), F32), ((4, F, R), F32), *HALVES, ((SLOTS, R), F32), ((8, R), F32)],
        schur_block, r, r_left, r_down, values, corners, *halves, *others,
        flops=MATMUL_FLOPS,
    )
    others = exchanged(*halves[:4])
    z1, message = call(
        operate_last_kernel,
        [((4, F, R), F32), ((8, R), F32)],
        inverse_block, spread_basis, corners, z0, residual, image, *halves, *others,
        flops=MATMUL_FLOPS,
    )
    near = lax.all_gather(message, NEAR)
    (spread_sums,) = call(sum_kernel, [((16, 8, R), F32)], near)
    sums = lax.all_to_all(spread_sums, FAR, 0, 0)
    (out,) = call(finish_kernel, [((2, 2 * F, R), F32)], z0, z1, scalars, sums)
    return out[:, None]


def solution(mesh):
    split = Mesh(mesh.devices.reshape(tuple(SPLIT.values())), tuple(SPLIT))
    four = P(BLK, CROSS, None, None)
    three = P(BLK, CROSS, None)
    return jax.shard_map(
        on_device,
        mesh=split,
        in_specs=(four, four, four, four, three, three, three, P(), P()),
        out_specs=four,
        check_vma=False,
    )
```

```python
import jax
import jax.numpy as jnp
import numpy as np
from jax import lax
from jax.experimental import pallas as pl
from jax.experimental.pallas import tpu as pltpu
from jax.sharding import Mesh
from jax.sharding import PartitionSpec as P

SPLIT = {"y": 4, "xl": 2, "xh": 2, "z": 8, "c": 2}
BLK = ("y", "xl")
CROSS = ("xh", "z", "c")
NEAR = ("z", "c")
FAR = ("y", "xl", "xh")
F = 256
R = 256
CORNERS = 512
EXACT = lax.Precision.HIGHEST
F32 = jnp.float32
BF16 = jnp.bfloat16

FACES = 7
PACK = F + 8
WEIGHT = F + 4
SIDES = ((4, 0, 6, 2), (5, 1, 2, 3))
OWNER = ((0, 0), (1, 0), (0, 0), (1, 0), (0, -1), (1, -1), (-1, 0))


def slot(axial, sector):
    return (axial + 1) * 3 + sector + 1


SLOTS = 16


def face_slots(face):
    axial, sector = OWNER[face]
    return [slot(axial + da, sector + ds) for da in (0, 1) for ds in (0, 1)]


class Fetched:
    def __init__(self, source, held, sems, pieces):
        self.held = held
        self.copies = {
            str(piece): pltpu.make_async_copy(source.at[piece], held.at[piece], sem)
            for piece, sem in zip(pieces, sems)
        }
        self.waited = set()

    def start(self):
        for copy in self.copies.values():
            copy.start()

    def get(self, piece=()):
        if str(piece) not in self.waited:
            self.waited.add(str(piece))
            self.copies[str(piece)].wait()
        return self.held.at[piece] if piece else self.held

    def finish(self):
        for piece, copy in self.copies.items():
            if piece not in self.waited:
                copy.wait()


class Stored:
    def __init__(self, held, target, sems, pieces):
        self.held = held
        self.copies = {
            str(piece): pltpu.make_async_copy(held.at[piece], target.at[piece], sem)
            for piece, sem in zip(pieces, sems)
        }

    def put(self, value, piece=()):
        self.held[piece if piece else ...] = value
        self.copies[str(piece)].start()

    def send(self, piece=()):
        self.copies[str(piece)].start()

    def finish(self):
        for copy in self.copies.values():
            copy.wait()


BLOCK_PIECES = [(k, slice(side * F, (side + 1) * F)) for k in range(2) for side in range(4)]


HALF_PIECES = [(k, slice(side * F, (side + 1) * F)) for k in range(2) for side in range(2)]


def pieces_of(shape):
    if shape == (2, 4 * F, 4 * F):
        return BLOCK_PIECES
    if shape == (2, 2 * F, R):
        return HALF_PIECES
    if len(shape) == 3 and shape[1:] in ((F, R), (PACK, R)):
        return [(k,) for k in range(shape[0])]
    return [()]


def block_piece(k, side):
    return BLOCK_PIECES[k * 4 + side]


class Here:
    def __init__(self, held):
        self.held = held

    def start(self):
        pass

    def get(self, piece=()):
        return self.held.at[piece] if piece else self.held

    def put(self, value, piece=()):
        self.held[piece if piece else ...] = value

    def send(self, piece=()):
        pass

    def finish(self):
        pass


def call(kernel, outs, *args, flops=0, smem=(), near=(), near_out=(), parts=None, scratch=()):
    size = sum(int(np.prod(a.shape)) * a.dtype.itemsize for a in args)
    size += sum(int(np.prod(s)) * jnp.dtype(d).itemsize for s, d in outs)
    inputs = [i for i in range(len(args)) if i not in smem]
    shapes = [(args[i].shape, args[i].dtype) for i in inputs] + list(outs)
    here = [i in near for i in inputs] + [i in near_out for i in range(len(outs))]
    pieces = [[] if there else pieces_of(shape) for (shape, _), there in zip(shapes, here)]
    for i, count in (parts or {}).items():
        pieces[i] = pieces[i][:count]
    staged = [shape for shape, there in zip(shapes, here) if not there]

    def body(*refs):
        operands, results = refs[: len(args)], refs[len(args) : len(args) + len(outs)]
        rest = list(refs[len(args) + len(outs) :])
        held, sems, rest = rest[: len(staged)], rest[len(staged)], rest[len(staged) + 1 :]
        made, at = [], 0
        for i, (ref, there) in enumerate(zip([operands[i] for i in inputs] + list(results), here)):
            if there:
                made.append(Here(ref))
                continue
            own = [sems.at[at + j] for j in range(len(pieces[i]))]
            at += len(own)
            vmem = held.pop(0)
            fetch = i < len(inputs)
            made.append(Fetched(ref, vmem, own, pieces[i]) if fetch else Stored(vmem, ref, own, pieces[i]))
        for operand in made[: len(inputs)]:
            operand.start()
        kernel(*[operands[i] for i in smem], *made, *rest)
        for array in made:
            array.finish()

    args = [a if i in smem or i in near else pltpu.with_memory_space_constraint(a, pltpu.HBM) for i, a in enumerate(args)]

    def space(there):
        return pl.BlockSpec(memory_space=pltpu.VMEM if there else pltpu.HBM)

    return pl.pallas_call(
        body,
        out_shape=[
            jax.ShapeDtypeStruct(s, d) if i in near_out else pltpu.HBM(s, d) for i, (s, d) in enumerate(outs)
        ],
        in_specs=[pl.BlockSpec(memory_space=pltpu.SMEM) if i in smem else space(i in near) for i in range(len(args))],
        out_specs=[space(i in near_out) for i in range(len(outs))],
        scratch_shapes=[pltpu.VMEM(s, d) for s, d in staged]
        + [pltpu.SemaphoreType.DMA((max(1, sum(len(p) for p in pieces)),)), *scratch],
        compiler_params=pltpu.CompilerParams(vmem_limit_bytes=32 * 1024 * 1024),
        cost_estimate=pl.CostEstimate(flops=flops, bytes_accessed=size, transcendentals=0),
    )(*args)


def thirds(value):
    high = value.astype(BF16)
    rest = value - high.astype(F32)
    middle = rest.astype(BF16)
    return high, middle, (rest - middle.astype(F32)).astype(BF16)


def nt(left, right):
    return lax.dot_general(left, right, (((1,), (1,)), ((), ())), preferred_element_type=F32)


def nn(left, right):
    return lax.dot_general(left, right, (((1,), (0,)), ((), ())), preferred_element_type=F32)


def weights_of(occ_ref, k):
    return 1.0 / (1.0 + occ_ref[k].astype(F32))


def pack_kernel(r, occ, basis, right, up):
    basis_ref, occ_ref = basis.get(), occ.get()

    def tail(k, part):
        spare = jnp.zeros((3, R), F32)
        return jnp.concatenate([basis_ref[k, :, part], weights_of(occ_ref, k)[:, part], spare], axis=0)

    first, last = slice(0, F), slice(F, 2 * F)
    right.held[0, F:, :] = tail(0, first)
    right.held[1, F:, :] = tail(1, first)
    up.held[F:, :] = tail(1, last)
    for k in range(2):
        right.held[k, :F, :] = own_face(r, k)
        right.send((k,))
    up.held[:F, :] = own_face(r, 3)
    up.send()


def loads_kernel(r, basis, out):
    basis_ref = basis.get()
    for piece in HALF_PIECES:
        r.get(piece)
    first = jnp.dot(basis_ref[0], r.held[0], precision=EXACT, preferred_element_type=F32)
    second = jnp.dot(basis_ref[1], r.held[1], precision=EXACT, preferred_element_type=F32)
    for peer in range(16):
        out.held[peer, 0:2, :] = first[0:2]
        out.held[peer, 2:4, :] = first[2:4] + second[0:2]
        out.held[peer, 4:6, :] = second[2:4]
        out.held[peer, 6:8, :] = jnp.zeros((2, R), F32)
    out.send()


def scale_column(row):
    eye = lax.broadcasted_iota(jnp.int32, (F, F), 1) == lax.broadcasted_iota(jnp.int32, (F, F), 0)
    return jnp.sum(jnp.where(eye, row, 0.0), axis=1, keepdims=True)


def placed(order_row):
    rows = lax.broadcasted_iota(jnp.int32, (F, F), 0)
    return jnp.where(order_row == rows, -1.0, 0.0).astype(BF16)


def reorder_block(s, out, work_ref, k, orders, weights):
    for row in range(4):
        rows = s.get(block_piece(k, row))
        for side in range(4):
            part = rows[:, side * F : (side + 1) * F]
            if orders[side] is not None:
                part = nt(part, orders[side])
            if weights[side] is not None:
                part = part.astype(F32) * weights[side]
            work_ref[:, side * F : (side + 1) * F] = part.astype(BF16)
        part = work_ref[...]
        if orders[row] is not None:
            part = nn(orders[row], part)
        if weights[row] is not None:
            part = part.astype(F32) * scale_column(weights[row])
        out.put(part.astype(BF16), block_piece(k, row))


def reorder_plain_kernel(s, left, down, out, work_ref):
    left_ref, down_ref = left.get(), down.get()
    for k in range(2):
        orders = (placed(left_ref[k]), None, placed(down_ref[k]), None)
        reorder_block(s, out, work_ref, k, orders, (None,) * 4)


def reorder_weighted_kernel(s, left, down, occ, out, work_ref):
    left_ref, down_ref, occ_ref = left.get(), down.get(), occ.get()
    first, second = weights_of(occ_ref, 0), weights_of(occ_ref, 1)
    for k, weight in enumerate((first, second)):
        orders = (placed(left_ref[k]), None, placed(down_ref[k]), None)
        below = None if k == 0 else first[:, F:]
        reorder_block(s, out, work_ref, k, orders, (None, weight[:, :F], below, weight[:, F:]))


def basis_kernel(basis, from_left, from_down, rows, columns, flat_ref):
    basis_ref, from_down_ref = basis.get(), from_down.get()
    sources = (
        basis_ref[0, :, :F],
        basis_ref[1, :, :F],
        basis_ref[0, :, F:],
        basis_ref[1, :, F:],
        from_left.get((0,))[F : F + 4, :],
        from_left.get((1,))[F : F + 4, :],
        from_down_ref[F : F + 4, :],
    )
    for face in range(FACES):
        flat_ref[...] = jnp.zeros_like(flat_ref)
        for k, row in enumerate(face_slots(face)):
            flat_ref[row : row + 1, :] = sources[face][k : k + 1, :]
        high, middle, low = thirds(flat_ref[...])
        rows.held[face, 0:16, :] = high
        rows.held[face, 16:32, :] = middle
        rows.held[face, 32:48, :] = low
        parts = [p.astype(F32) for p in (high, high, high, middle, middle, low)]
        parts.append(jnp.zeros((32, F), F32))
        columns.held[face] = jnp.concatenate(parts, axis=0).T.astype(BF16)
    rows.send()
    columns.send()


def corner_onehot(numbers_t, axial, sector, spare):
    wanted = (axial & 15) * 32 + (sector & 31)
    columns = lax.broadcasted_iota(jnp.int32, (wanted.shape[0], CORNERS), 1)
    picks = jnp.where((columns == wanted) & jnp.logical_not(spare), 1.0, 0.0).astype(BF16)
    return nt(picks, numbers_t).astype(BF16)


def coarse_block_kernel(place_ref, numbers, inverse, first, later):
    blk, xh, near = place_ref[0], place_ref[1], place_ref[2]
    ids = lax.broadcasted_iota(jnp.int32, (CORNERS, CORNERS), 0)
    numbers_t = jnp.where(numbers.get()[...] == ids, 1.0, 0.0).astype(BF16)
    rows = lax.broadcasted_iota(jnp.int32, (16 * SLOTS, 1), 0)
    peer = rows >> 4
    entry = rows & 15
    third = (entry >= 3).astype(jnp.int32) + (entry >= 6).astype(jnp.int32) + (entry >= 9).astype(jnp.int32)
    da = third - 1
    ds = entry - 3 * third - 1
    spare = entry >= 12
    far_rows = corner_onehot(numbers_t, 2 * (peer >> 1) + da, (peer & 1) * 16 + near + ds, spare)
    near_rows = corner_onehot(numbers_t, 2 * blk + da, xh * 16 + peer + ds, spare)
    few = lax.broadcasted_iota(jnp.int32, (16 * 8, 1), 0)
    own = few & 7
    own_rows = corner_onehot(numbers_t, 2 * blk + (own >> 1), xh * 16 + (few >> 3) + (own & 1), own >= 6)
    picked = thirds(sum(nn(far_rows, part) for part in thirds(inverse.get()[...])[::-1]))[::-1]
    first.put(sum(nt(part, own_rows) for part in picked))
    block = sum(nt(part, near_rows) for part in picked)
    columns = lax.broadcasted_iota(jnp.int32, (16 * SLOTS, 16 * SLOTS), 1) & 15
    passed = (columns == entry) & spare
    later.put(jnp.where(passed, 1.0, block))


HALVES = [((2, F, R), F32), ((2, F, R), F32), ((F, R), F32), ((F, R), F32), ((F, R), F32)]


def apply_block(s, operand_ref, left, right, up, down, mid, weights=None):
    def outer(value, which):
        return value if weights is None else value * weights[which]

    for k in range(2):
        sides = [nn(s.get(block_piece(k, side))[...], operand_ref[k]) for side in range(4)]
        left.put(outer(sides[0], k), (k,))
        right.put(sides[1], (k,))
        if k == 0:
            down.put(outer(sides[2], 2))
            shared = sides[3]
        else:
            mid.put(shared + sides[2])
            up.put(sides[3])


def set_operand(operand_ref, face, value):
    value = value.astype(BF16)
    for k in range(2):
        for side in range(4):
            if SIDES[k][side] == face:
                operand_ref[k, side * F : (side + 1) * F, :] = value


def outer_weights(from_left, from_down):
    rows = [from_left.get((k,))[WEIGHT : WEIGHT + 1, :] for k in range(2)]
    rows.append(from_down.get()[WEIGHT : WEIGHT + 1, :])
    return [scale_column(row) for row in rows]


def first_kernel(
    left_order, down_order, occ, s, r, from_left, from_down,
    block, left, right, up, down, mid, operand_ref, strip_ref,
):
    reorder_weighted_kernel(s, left_order, down_order, occ, block, strip_ref)
    weights = outer_weights(from_left, from_down)
    for k in range(2):
        set_operand(operand_ref, k, own_face(r, k))
        set_operand(operand_ref, 2 + k, own_face(r, 2 + k))
        set_operand(operand_ref, 4 + k, from_left.get((k,))[:F, :] * weights[k])
    set_operand(operand_ref, 6, from_down.get()[:F, :] * weights[2])
    apply_block(Here(block.held), operand_ref, left, right, up, down, mid, weights)


PLACES = ((1, (0,)), (1, (1,)), (4, ()), (2, ()), (0, (0,)), (0, (1,)), (3, ()))


def own_share(halves, face):
    which, piece = PLACES[face]
    return halves[which].get(piece)[...]


def own_image(halves, face):
    which, piece = PLACES[face]
    return halves[which].held[piece if piece else ...]


def assembled(halves, others, face):
    which, piece = PLACES[face]
    if which == 4:
        return own_share(halves, face)
    return own_share(halves, face) + others[which].get(piece)[...]


def stacked(values):
    high, middle, low = thirds(values)
    parts = [high, middle, low, high, middle, high, jnp.zeros((32, R), BF16)]
    return jnp.concatenate(parts, axis=0)


def face_loads(rows_ref, face, image):
    out = sum(nn(rows_ref[face], part) for part in thirds(image)[1::-1])
    return out[32:48] + out[16:32] + out[0:16]


def face_piece(face):
    return HALF_PIECES[(face % 2) * 2 + face // 2]


def own_face(r, face):
    return r.get(face_piece(face))[...]


def total(value):
    return jnp.sum(value, axis=0, keepdims=True)


def operate_first_kernel(
    values, columns, l0, r0, u0, d0, m0, fl, fr, fu, fd, r, s, rows,
    z, left, right, up, down, mid, message, corners_out, operand_ref,
):
    corners = jnp.sum(values.get()[...], axis=0)
    corners_out.put(corners)
    terms = stacked(corners)
    columns_ref = columns.get()
    before, others = (l0, r0, u0, d0, m0), (fl, fr, fu, fd)
    images = (left, right, up, down, mid)
    progress = jnp.zeros((1, R), F32)
    for face in range(FACES):
        value = assembled(before, others, face) + nn(columns_ref[face], terms)
        z.put(value, (face,))
        set_operand(operand_ref, face, value)
        if face < 4:
            progress = progress + total(own_face(r, face) * value)
    apply_block(s, operand_ref, *images)
    rows_ref = rows.get()
    loads = jnp.zeros((SLOTS, R), F32)
    curvature = jnp.zeros((1, R), F32)
    for face in range(FACES):
        image = own_image(images, face)
        loads = loads + face_loads(rows_ref, face, image)
        curvature = curvature + total(z.held[face] * image)
    for peer in range(16):
        message.held[peer] = loads
        message.held[peer, 12:13, :] = progress
        message.held[peer, 13:14, :] = curvature
    message.send()


def second_kernel(
    values, corners_before, r_left, r_down, r, l0, r0, u0, d0, m0, fl, fr, fu, fd, s,
    residual, image_out, left, right, up, down, mid, corners_out, scalars, operand_ref,
):
    sums = jnp.sum(values.get()[...], axis=0)
    progress, curvature = sums[12:13, :], sums[13:14, :]
    alpha = progress / curvature
    corners_out.put(corners_before.get()[...] - alpha * sums)
    scalars.held[...] = jnp.zeros((8, R), F32)
    scalars.held[0:1, :] = progress
    scalars.held[1:2, :] = curvature
    scalars.held[2:3, :] = alpha
    scalars.send()
    before, others = (l0, r0, u0, d0, m0), (fl, fr, fu, fd)
    weights = outer_weights(r_left, r_down)
    for face in range(FACES):
        image = assembled(before, others, face)
        if face < 4:
            start = own_face(r, face)
        elif face < 6:
            start = r_left.get((face - 4,))[:F, :]
        else:
            start = r_down.get()[:F, :]
        value = start - alpha * image
        if face < 4:
            image_out.put(image, (face,))
            residual.put(value, (face,))
        else:
            value = value * weights[face - 4]
        set_operand(operand_ref, face, value)
    apply_block(s, operand_ref, left, right, up, down, mid, weights)


def operate_last_kernel(
    corners_in, columns, l0, r0, u0, d0, m0, fl, fr, fu, fd, residual, image_in, s, z0,
    z, message, operand_ref, z_ref,
):
    corners = corners_in.get()[...]
    terms = stacked(jnp.where(lax.broadcasted_iota(jnp.int32, corners.shape, 0) < 12, corners, 0.0))
    columns_ref = columns.get()
    before, others = (l0, r0, u0, d0, m0), (fl, fr, fu, fd)
    progress = jnp.zeros((1, R), F32)
    mixed = jnp.zeros((1, R), F32)
    for face in range(FACES):
        value = assembled(before, others, face) + nn(columns_ref[face], terms)
        z_ref[face] = value
        set_operand(operand_ref, face, value)
        if face < 4:
            z.put(value, (face,))
            progress = progress + total(residual.get((face,))[...] * value)
            mixed = mixed + total(image_in.get((face,))[...] * value)
    curvature = jnp.zeros((1, R), F32)
    for k in range(2):
        for side in range(4):
            image = nn(s.get(block_piece(k, side))[...], operand_ref[k])
            face = SIDES[k][side]
            curvature = curvature + total(z_ref[face] * image)
            mixed = mixed + total(z0.get((face,))[...] * image)
    for peer in range(16):
        message.held[peer, 0:1, :] = progress
        message.held[peer, 1:2, :] = curvature
        message.held[peer, 2:3, :] = mixed
        message.held[peer, 3:4, :] = jnp.zeros((1, R), F32)
    message.send()


def finish_kernel(sums_in, scalars, z0, z1, out):
    sums = jnp.sum(sums_in.get()[...], axis=0)
    progress, curvature, mixed = sums[0:1, :], sums[1:2, :], sums[2:3, :]
    before = scalars.get()[...]
    first_progress, first_curvature, alpha = before[0:1, :], before[1:2, :], before[2:3, :]
    ratio = progress / first_progress
    last = progress / (curvature + ratio * (mixed + ratio * first_curvature))
    scale0 = alpha + last * ratio
    for face in (0, 2, 1, 3):
        out.put(scale0 * z0.get((face,))[...] + last * z1.get((face,))[...], face_piece(face))


def partial_kernel(message, block, out):
    flat = jnp.concatenate([message.get()[i] for i in range(16)], axis=0)
    values = jnp.dot(block.get()[...], flat, precision=EXACT, preferred_element_type=F32)
    for i in range(16):
        out.held[i] = values[i * SLOTS : (i + 1) * SLOTS]
    out.send()


def sum_kernel(near, out):
    sums = jnp.sum(near.get()[...], axis=0)
    for i in range(16):
        out.held[i] = sums
    out.send()


def moved(block, axes, count, distance):
    return lax.ppermute(block, axes, [(i, (i + distance) % count) for i in range(count)])


def exchanged(left, right, up, down):
    return (
        moved(right, CROSS, 32, 1),
        moved(left, CROSS, 32, -1),
        moved(down, BLK, 8, -1),
        moved(up, BLK, 8, 1),
    )


MATMUL_FLOPS = 2 * 2 * (4 * F) * (4 * F) * R


def on_device(r, s_inverse, s, basis, occ, left_order, down_order, numbers, coarse_inverse):
    r, s_inverse, s, basis = r[:, 0], s_inverse[:, 0], s[:, 0], basis[:, 0]
    place = jnp.stack([lax.axis_index(BLK), lax.axis_index("xh"), lax.axis_index(NEAR)]).astype(jnp.int32)
    operand = pltpu.VMEM((2, 4 * F, R), BF16)
    strip = pltpu.VMEM((F, 4 * F), BF16)

    right, up = call(pack_kernel, [((2, PACK, R), F32), ((PACK, R), F32)], r, occ, basis)
    r_left = moved(right, CROSS, 32, 1)
    r_down = moved(up, BLK, 8, 1)
    (loads,) = call(loads_kernel, [((16, 8, R), F32)], r, basis)
    near = lax.all_to_all(loads, NEAR, 0, 0)
    first_block, later_block = call(
        coarse_block_kernel,
        [((16 * SLOTS, 16 * 8), F32), ((16 * SLOTS, 16 * SLOTS), F32)],
        place, numbers[None, :], coarse_inverse,
        smem=(0,),
    )
    (inverse_block,) = call(
        reorder_plain_kernel,
        [(s_inverse.shape, BF16)],
        s_inverse, left_order, down_order,
        flops=2 * MATMUL_FLOPS, scratch=[strip],
    )
    r_left, r_down, first_block, later_block, inverse_block = lax.optimization_barrier(
        (r_left, r_down, first_block, later_block, inverse_block)
    )

    schur_block, *halves = call(
        first_kernel,
        [(s.shape, BF16), *HALVES],
        left_order, down_order, occ, s, r, r_left, r_down,
        flops=3 * MATMUL_FLOPS, near=(5, 6), scratch=[operand, strip],
    )
    near, *halves = lax.optimization_barrier((near, *halves))
    others = exchanged(*halves[:4])
    (partial,) = call(partial_kernel, [((16, SLOTS, R), F32)], near, first_block, near=(0,))
    values = lax.all_to_all(partial, FAR, 0, 0)
    rows, columns = call(
        basis_kernel,
        [((FACES, 48, F), BF16), ((FACES, F, 128), BF16)],
        basis, r_left, r_down,
        scratch=[pltpu.VMEM((SLOTS, F), F32)],
    )
    z0, *halves, message, corners = call(
        operate_first_kernel,
        [((FACES, F, R), F32), *HALVES, ((16, SLOTS, R), F32), ((SLOTS, R), F32)],
        values, columns, *halves, *others, r, inverse_block, rows,
        flops=MATMUL_FLOPS, near=(0, 7, 8, 9, 10), scratch=[operand],
    )
    others = exchanged(*halves[:4])
    near = lax.all_to_all(message, NEAR, 0, 0)
    (partial,) = call(partial_kernel, [((16, SLOTS, R), F32)], near, later_block, near=(0,))
    values = lax.all_to_all(partial, FAR, 0, 0)
    residual, image, *halves, corners, scalars = call(
        second_kernel,
        [((4, F, R), F32), ((4, F, R), F32), *HALVES, ((SLOTS, R), F32), ((8, R), F32)],
        values, corners, r_left, r_down, r, *halves, *others, schur_block,
        flops=MATMUL_FLOPS, near=(0, 10, 11, 12, 13), near_out=(0, 1, 2, 3, 4, 5, 6, 7), scratch=[operand],
    )
    others = exchanged(*halves[:4])
    z1, message = call(
        operate_last_kernel,
        [((4, F, R), F32), ((16, 4, R), F32)],
        corners, columns, *halves, *others, residual, image, inverse_block, z0,
        flops=MATMUL_FLOPS, near=tuple(range(15)), scratch=[operand, pltpu.VMEM((FACES, F, R), F32)],
    )
    near = lax.all_to_all(message, NEAR, 0, 0)
    (spread_sums,) = call(sum_kernel, [((16, 4, R), F32)], near, near=(0,))
    sums = lax.all_to_all(spread_sums, FAR, 0, 0)
    (out,) = call(finish_kernel, [((2, 2 * F, R), F32)], sums, scalars, z0, z1, near=(0,), parts={2: 4})
    return out[:, None]


def solution(mesh):
    split = Mesh(mesh.devices.reshape(tuple(SPLIT.values())), tuple(SPLIT))
    four = P(BLK, CROSS, None, None)
    three = P(BLK, CROSS, None)
    return jax.shard_map(
        on_device,
        mesh=split,
        in_specs=(four, four, four, four, three, three, three, P(), P()),
        out_specs=four,
        check_vma=False,
    )
```

```python
import jax
import jax.numpy as jnp
import numpy as np
from jax import lax
from jax.experimental import pallas as pl
from jax.experimental.pallas import tpu as pltpu
from jax.sharding import Mesh
from jax.sharding import PartitionSpec as P

SPLIT = {"y": 4, "xl": 2, "xh": 2, "z": 8, "c": 2}
BLK = ("y", "xl")
CROSS = ("xh", "z", "c")
NEAR = ("z", "c")
FAR = ("y", "xl", "xh")
F = 256
R = 256
CORNERS = 512
EXACT = lax.Precision.HIGHEST
F32 = jnp.float32
BF16 = jnp.bfloat16

FACES = 7
PACK = F + 8
WEIGHT = F + 4
SIDES = ((4, 0, 6, 2), (5, 1, 2, 3))
OWNER = ((0, 0), (1, 0), (0, 0), (1, 0), (0, -1), (1, -1), (-1, 0))


def slot(axial, sector):
    return (axial + 1) * 3 + sector + 1


SLOTS = 16


def face_slots(face):
    axial, sector = OWNER[face]
    return [slot(axial + da, sector + ds) for da in (0, 1) for ds in (0, 1)]


class Fetched:
    def __init__(self, source, held, sems, pieces):
        self.held = held
        self.copies = {
            str(piece): pltpu.make_async_copy(source.at[piece], held.at[piece], sem)
            for piece, sem in zip(pieces, sems)
        }
        self.waited = set()

    def start(self):
        for copy in self.copies.values():
            copy.start()

    def get(self, piece=()):
        if str(piece) not in self.waited:
            self.waited.add(str(piece))
            self.copies[str(piece)].wait()
        return self.held.at[piece] if piece else self.held

    def finish(self):
        for piece, copy in self.copies.items():
            if piece not in self.waited:
                copy.wait()


class Stored:
    def __init__(self, held, target, sems, pieces):
        self.held = held
        self.copies = {
            str(piece): pltpu.make_async_copy(held.at[piece], target.at[piece], sem)
            for piece, sem in zip(pieces, sems)
        }

    def put(self, value, piece=()):
        self.held[piece if piece else ...] = value
        self.copies[str(piece)].start()

    def send(self, piece=()):
        self.copies[str(piece)].start()

    def finish(self):
        for copy in self.copies.values():
            copy.wait()


BLOCK_PIECES = [(k, slice(side * F, (side + 1) * F)) for k in range(2) for side in range(4)]


HALF_PIECES = [(k, slice(side * F, (side + 1) * F)) for k in range(2) for side in range(2)]


def pieces_of(shape):
    if shape == (2, 4 * F, 4 * F):
        return BLOCK_PIECES
    if shape == (2, 2 * F, R):
        return HALF_PIECES
    if len(shape) == 3 and shape[1:] in ((F, R), (PACK, R)):
        return [(k,) for k in range(shape[0])]
    return [()]


def block_piece(k, side):
    return BLOCK_PIECES[k * 4 + side]


class Here:
    def __init__(self, held):
        self.held = held

    def start(self):
        pass

    def get(self, piece=()):
        return self.held.at[piece] if piece else self.held

    def put(self, value, piece=()):
        self.held[piece if piece else ...] = value

    def send(self, piece=()):
        pass

    def finish(self):
        pass


def call(kernel, outs, *args, flops=0, smem=(), near=(), near_out=(), parts=None, scratch=()):
    size = sum(int(np.prod(a.shape)) * a.dtype.itemsize for a in args)
    size += sum(int(np.prod(s)) * jnp.dtype(d).itemsize for s, d in outs)
    inputs = [i for i in range(len(args)) if i not in smem]
    shapes = [(args[i].shape, args[i].dtype) for i in inputs] + list(outs)
    here = [i in near for i in inputs] + [i in near_out for i in range(len(outs))]
    pieces = [[] if there else pieces_of(shape) for (shape, _), there in zip(shapes, here)]
    for i, count in (parts or {}).items():
        pieces[i] = pieces[i][:count]
    staged = [shape for shape, there in zip(shapes, here) if not there]

    def body(*refs):
        operands, results = refs[: len(args)], refs[len(args) : len(args) + len(outs)]
        rest = list(refs[len(args) + len(outs) :])
        held, sems, rest = rest[: len(staged)], rest[len(staged)], rest[len(staged) + 1 :]
        made, at = [], 0
        for i, (ref, there) in enumerate(zip([operands[i] for i in inputs] + list(results), here)):
            if there:
                made.append(Here(ref))
                continue
            own = [sems.at[at + j] for j in range(len(pieces[i]))]
            at += len(own)
            vmem = held.pop(0)
            fetch = i < len(inputs)
            made.append(Fetched(ref, vmem, own, pieces[i]) if fetch else Stored(vmem, ref, own, pieces[i]))
        for operand in made[: len(inputs)]:
            operand.start()
        kernel(*[operands[i] for i in smem], *made, *rest)
        for array in made:
            array.finish()

    args = [a if i in smem or i in near else pltpu.with_memory_space_constraint(a, pltpu.HBM) for i, a in enumerate(args)]

    def space(there):
        return pl.BlockSpec(memory_space=pltpu.VMEM if there else pltpu.HBM)

    return pl.pallas_call(
        body,
        out_shape=[
            jax.ShapeDtypeStruct(s, d) if i in near_out else pltpu.HBM(s, d) for i, (s, d) in enumerate(outs)
        ],
        in_specs=[pl.BlockSpec(memory_space=pltpu.SMEM) if i in smem else space(i in near) for i in range(len(args))],
        out_specs=[space(i in near_out) for i in range(len(outs))],
        scratch_shapes=[pltpu.VMEM(s, d) for s, d in staged]
        + [pltpu.SemaphoreType.DMA((max(1, sum(len(p) for p in pieces)),)), *scratch],
        compiler_params=pltpu.CompilerParams(vmem_limit_bytes=32 * 1024 * 1024),
        cost_estimate=pl.CostEstimate(flops=0, bytes_accessed=0, transcendentals=0),
    )(*args)


def thirds(value):
    high = value.astype(BF16)
    rest = value - high.astype(F32)
    middle = rest.astype(BF16)
    return high, middle, (rest - middle.astype(F32)).astype(BF16)


def nt(left, right):
    return lax.dot_general(left, right, (((1,), (1,)), ((), ())), preferred_element_type=F32)


def nn(left, right):
    return lax.dot_general(left, right, (((1,), (0,)), ((), ())), preferred_element_type=F32)


def weights_of(occ_ref, k):
    return 1.0 / (1.0 + occ_ref[k].astype(F32))


def pack_kernel(r, occ, basis, right, up):
    basis_ref, occ_ref = basis.get(), occ.get()

    def tail(k, part):
        spare = jnp.zeros((3, R), F32)
        return jnp.concatenate([basis_ref[k, :, part], weights_of(occ_ref, k)[:, part], spare], axis=0)

    first, last = slice(0, F), slice(F, 2 * F)
    right.held[0, F:, :] = tail(0, first)
    right.held[1, F:, :] = tail(1, first)
    up.held[F:, :] = tail(1, last)
    for k in range(2):
        right.held[k, :F, :] = own_face(r, k)
        right.send((k,))
    up.held[:F, :] = own_face(r, 3)
    up.send()


def loads_kernel(r, basis, out):
    basis_ref = basis.get()
    for piece in HALF_PIECES:
        r.get(piece)
    first = jnp.dot(basis_ref[0], r.held[0], precision=EXACT, preferred_element_type=F32)
    second = jnp.dot(basis_ref[1], r.held[1], precision=EXACT, preferred_element_type=F32)
    for peer in range(16):
        out.held[peer, 0:2, :] = first[0:2]
        out.held[peer, 2:4, :] = first[2:4] + second[0:2]
        out.held[peer, 4:6, :] = second[2:4]
        out.held[peer, 6:8, :] = jnp.zeros((2, R), F32)
    out.send()


def scale_column(row):
    eye = lax.broadcasted_iota(jnp.int32, (F, F), 1) == lax.broadcasted_iota(jnp.int32, (F, F), 0)
    return jnp.sum(jnp.where(eye, row, 0.0), axis=1, keepdims=True)


def placed(order_row):
    rows = lax.broadcasted_iota(jnp.int32, (F, F), 0)
    return jnp.where(order_row == rows, -1.0, 0.0).astype(BF16)


def reorder_block(s, outs, work_ref, k, orders, weights):
    for row in range(4):
        rows = s.get(block_piece(k, row))
        for side in range(4):
            part = rows[:, side * F : (side + 1) * F]
            if orders[side] is not None:
                part = nt(part, orders[side])
            if weights[side] is not None:
                part = part.astype(F32) * weights[side]
            work_ref[:, side * F : (side + 1) * F] = part.astype(BF16)
        part = work_ref[...]
        if orders[row] is not None:
            part = nn(orders[row], part)
        if weights[row] is not None:
            part = part.astype(F32) * scale_column(weights[row])
        for out in outs:
            out.put(part.astype(BF16), block_piece(k, row))


def reorder_plain_kernel(s, left, down, out, work_ref):
    left_ref, down_ref = left.get(), down.get()
    for k in range(2):
        orders = (placed(left_ref[k]), None, placed(down_ref[k]), None)
        reorder_block(s, (out,), work_ref, k, orders, (None,) * 4)


def reorder_weighted_kernel(s, left, down, occ, out, twin, work_ref):
    left_ref, down_ref, occ_ref = left.get(), down.get(), occ.get()
    first, second = weights_of(occ_ref, 0), weights_of(occ_ref, 1)
    for k, weight in enumerate((first, second)):
        orders = (placed(left_ref[k]), None, placed(down_ref[k]), None)
        below = None if k == 0 else first[:, F:]
        reorder_block(s, (out, twin), work_ref, k, orders, (None, weight[:, :F], below, weight[:, F:]))


def basis_kernel(basis, from_left, from_down, rows, columns, flat_ref):
    basis_ref, from_down_ref = basis.get(), from_down.get()
    sources = (
        basis_ref[0, :, :F],
        basis_ref[1, :, :F],
        basis_ref[0, :, F:],
        basis_ref[1, :, F:],
        from_left.get((0,))[F : F + 4, :],
        from_left.get((1,))[F : F + 4, :],
        from_down_ref[F : F + 4, :],
    )
    for face in range(FACES):
        flat_ref[...] = jnp.zeros_like(flat_ref)
        for k, row in enumerate(face_slots(face)):
            flat_ref[row : row + 1, :] = sources[face][k : k + 1, :]
        high, middle, low = thirds(flat_ref[...])
        rows.held[face, 0:16, :] = high
        rows.held[face, 16:32, :] = middle
        rows.held[face, 32:48, :] = low
        parts = [p.astype(F32) for p in (high, high, high, middle, middle, low)]
        parts.append(jnp.zeros((32, F), F32))
        columns.held[face] = jnp.concatenate(parts, axis=0).T.astype(BF16)
    rows.send()
    columns.send()


def corner_onehot(numbers_t, axial, sector, spare):
    wanted = (axial & 15) * 32 + (sector & 31)
    columns = lax.broadcasted_iota(jnp.int32, (wanted.shape[0], CORNERS), 1)
    picks = jnp.where((columns == wanted) & jnp.logical_not(spare), 1.0, 0.0).astype(BF16)
    return nt(picks, numbers_t).astype(BF16)


def coarse_block_kernel(place_ref, numbers, inverse, first, later):
    blk, xh, near = place_ref[0], place_ref[1], place_ref[2]
    ids = lax.broadcasted_iota(jnp.int32, (CORNERS, CORNERS), 0)
    numbers_t = jnp.where(numbers.get()[...] == ids, 1.0, 0.0).astype(BF16)
    rows = lax.broadcasted_iota(jnp.int32, (16 * SLOTS, 1), 0)
    peer = rows >> 4
    entry = rows & 15
    third = (entry >= 3).astype(jnp.int32) + (entry >= 6).astype(jnp.int32) + (entry >= 9).astype(jnp.int32)
    da = third - 1
    ds = entry - 3 * third - 1
    spare = entry >= 12
    far_rows = corner_onehot(numbers_t, 2 * (peer >> 1) + da, (peer & 1) * 16 + near + ds, spare)
    near_rows = corner_onehot(numbers_t, 2 * blk + da, xh * 16 + peer + ds, spare)
    few = lax.broadcasted_iota(jnp.int32, (16 * 8, 1), 0)
    source, own = few >> 3, few & 7
    own_rows = corner_onehot(
        numbers_t, 2 * (source >> 1) + (own >> 1), (source & 1) * 16 + near + (own & 1), own >= 6
    )
    terms = thirds(inverse.get()[...])[::-1]
    picked = thirds(sum(nn(near_rows, part) for part in terms))[::-1]
    first.put(sum(nt(part, own_rows) for part in picked))
    block = sum(nt(part, far_rows) for part in picked)
    columns = lax.broadcasted_iota(jnp.int32, (16 * SLOTS, 16 * SLOTS), 1) & 15
    passed = (columns == entry) & spare
    later.put(jnp.where(passed, 1.0, block))


HALVES = [((2, F, R), F32), ((2, F, R), F32), ((F, R), F32), ((F, R), F32), ((F, R), F32)]


def apply_block(s, operand_ref, left, right, up, down, mid, weights=None, seen=None):
    stores = {
        0: lambda v: right.put(v, (0,)),
        1: lambda v: right.put(v, (1,)),
        2: mid.put,
        3: up.put,
        4: lambda v: left.put(v, (0,)),
        5: lambda v: left.put(v, (1,)),
        6: down.put,
    }
    shared = None
    for k in range(2):
        for side in range(4):
            face = SIDES[k][side]
            image = nn(s.get(block_piece(k, side))[...], operand_ref[k])
            if face == 2:
                if shared is None:
                    shared = image
                    continue
                image = shared + image
            if weights is not None and face >= 4:
                image = image * weights[face - 4]
            stores[face](image)
            if seen is not None:
                seen(face, image)


def set_operand(operand_ref, face, value):
    value = value.astype(BF16)
    for k in range(2):
        for side in range(4):
            if SIDES[k][side] == face:
                operand_ref[k, side * F : (side + 1) * F, :] = value


def outer_weights(from_left, from_down):
    rows = [from_left.get((k,))[WEIGHT : WEIGHT + 1, :] for k in range(2)]
    rows.append(from_down.get()[WEIGHT : WEIGHT + 1, :])
    return [scale_column(row) for row in rows]


def first_kernel(r, from_left, from_down, s, left, right, up, down, mid, operand_ref):
    weights = outer_weights(from_left, from_down)
    set_operand(operand_ref, 6, from_down.get()[:F, :] * weights[2])
    for k in range(2):
        set_operand(operand_ref, 4 + k, from_left.get((k,))[:F, :] * weights[k])
    for face in range(4):
        set_operand(operand_ref, face, own_face(r, face))
    apply_block(s, operand_ref, left, right, up, down, mid, weights)


PLACES = ((1, (0,)), (1, (1,)), (4, ()), (2, ()), (0, (0,)), (0, (1,)), (3, ()))


def own_share(halves, face):
    which, piece = PLACES[face]
    return halves[which].get(piece)[...]


def assembled(halves, others, face):
    which, piece = PLACES[face]
    if which == 4:
        return own_share(halves, face)
    return own_share(halves, face) + others[which].get(piece)[...]


def stacked(values):
    high, middle, low = thirds(values)
    parts = [high, middle, low, high, middle, high, jnp.zeros((32, R), BF16)]
    return jnp.concatenate(parts, axis=0)


def face_loads(rows_ref, face, image):
    out = sum(nn(rows_ref[face], part) for part in thirds(image)[1::-1])
    return out[32:48] + out[16:32] + out[0:16]


def face_piece(face):
    return HALF_PIECES[(face % 2) * 2 + face // 2]


def own_face(r, face):
    return r.get(face_piece(face))[...]


def total(value):
    return jnp.sum(value, axis=0, keepdims=True)


def operate_first_kernel(
    values, columns, l0, r0, u0, d0, m0, fl, fr, fu, fd, r, rows, s,
    z, left, right, up, down, mid, message, corners_out, operand_ref,
):
    corners = jnp.sum(values.get()[...], axis=0)
    corners_out.put(corners)
    terms = stacked(corners)
    columns_ref = columns.get()
    before, others = (l0, r0, u0, d0, m0), (fl, fr, fu, fd)
    images = (left, right, up, down, mid)
    progress = jnp.zeros((1, R), F32)
    for face in range(FACES):
        value = assembled(before, others, face) + nn(columns_ref[face], terms)
        z.put(value, (face,))
        set_operand(operand_ref, face, value)
        if face < 4:
            progress = progress + total(own_face(r, face) * value)
    rows_ref = rows.get()
    sums = [jnp.zeros((SLOTS, R), F32), jnp.zeros((1, R), F32)]

    def seen(face, image):
        sums[0] = sums[0] + face_loads(rows_ref, face, image)
        sums[1] = sums[1] + total(z.held[face] * image)

    apply_block(s, operand_ref, *images, seen=seen)
    loads, curvature = sums
    for peer in range(16):
        message.held[peer] = loads
        message.held[peer, 12:13, :] = progress
        message.held[peer, 13:14, :] = curvature
    message.send()


def second_kernel(
    values, corners_before, r_left, r_down, r, l0, r0, u0, d0, m0, fl, fr, fu, fd, s,
    residual, image_out, left, right, up, down, mid, corners_out, scalars, operand_ref,
):
    sums = jnp.sum(values.get()[...], axis=0)
    progress, curvature = sums[12:13, :], sums[13:14, :]
    alpha = progress / curvature
    corners_out.put(corners_before.get()[...] - alpha * sums)
    scalars.held[...] = jnp.zeros((8, R), F32)
    scalars.held[0:1, :] = progress
    scalars.held[1:2, :] = curvature
    scalars.held[2:3, :] = alpha
    scalars.send()
    before, others = (l0, r0, u0, d0, m0), (fl, fr, fu, fd)
    weights = outer_weights(r_left, r_down)
    for face in range(FACES):
        image = assembled(before, others, face)
        if face < 4:
            start = own_face(r, face)
        elif face < 6:
            start = r_left.get((face - 4,))[:F, :]
        else:
            start = r_down.get()[:F, :]
        value = start - alpha * image
        if face < 4:
            image_out.put(image, (face,))
            residual.put(value, (face,))
        else:
            value = value * weights[face - 4]
        set_operand(operand_ref, face, value)
    apply_block(s, operand_ref, left, right, up, down, mid, weights)


def operate_last_kernel(
    corners_in, columns, l0, r0, u0, d0, m0, fl, fr, fu, fd, residual, image_in, s, z0,
    z, message, operand_ref, z_ref,
):
    corners = corners_in.get()[...]
    terms = stacked(jnp.where(lax.broadcasted_iota(jnp.int32, corners.shape, 0) < 12, corners, 0.0))
    columns_ref = columns.get()
    before, others = (l0, r0, u0, d0, m0), (fl, fr, fu, fd)
    progress = jnp.zeros((1, R), F32)
    mixed = jnp.zeros((1, R), F32)
    for face in range(FACES):
        value = assembled(before, others, face) + nn(columns_ref[face], terms)
        z_ref[face] = value
        set_operand(operand_ref, face, value)
        if face < 4:
            z.put(value, (face,))
            progress = progress + total(residual.get((face,))[...] * value)
            mixed = mixed + total(image_in.get((face,))[...] * value)
    curvature = jnp.zeros((1, R), F32)
    for k in range(2):
        for side in range(4):
            image = nn(s.get(block_piece(k, side))[...], operand_ref[k])
            face = SIDES[k][side]
            curvature = curvature + total(z_ref[face] * image)
            mixed = mixed + total(z0.get((face,))[...] * image)
    for peer in range(16):
        message.held[peer, 0:1, :] = progress
        message.held[peer, 1:2, :] = curvature
        message.held[peer, 2:3, :] = mixed
        message.held[peer, 3:4, :] = jnp.zeros((1, R), F32)
    message.send()


def finish_kernel(sums_in, scalars, z0, z1, out):
    sums = jnp.sum(sums_in.get()[...], axis=0)
    progress, curvature, mixed = sums[0:1, :], sums[1:2, :], sums[2:3, :]
    before = scalars.get()[...]
    first_progress, first_curvature, alpha = before[0:1, :], before[1:2, :], before[2:3, :]
    ratio = progress / first_progress
    last = progress / (curvature + ratio * (mixed + ratio * first_curvature))
    scale0 = alpha + last * ratio
    for face in (0, 2, 1, 3):
        out.put(scale0 * z0.get((face,))[...] + last * z1.get((face,))[...], face_piece(face))


def partial_kernel(message, block, out):
    flat = jnp.concatenate([message.get()[i] for i in range(16)], axis=0)
    values = jnp.dot(block.get()[...], flat, precision=EXACT, preferred_element_type=F32)
    for i in range(16):
        out.held[i] = values[i * SLOTS : (i + 1) * SLOTS]
    out.send()


def sum_kernel(near, out):
    sums = jnp.sum(near.get()[...], axis=0)
    for i in range(16):
        out.held[i] = sums
    out.send()


def moved(block, axes, count, distance):
    return lax.ppermute(block, axes, [(i, (i + distance) % count) for i in range(count)])


def exchanged(left, right, up, down):
    return (
        moved(right, CROSS, 32, 1),
        moved(left, CROSS, 32, -1),
        moved(down, BLK, 8, -1),
        moved(up, BLK, 8, 1),
    )


MATMUL_FLOPS = 2 * 2 * (4 * F) * (4 * F) * R


def on_device(r, s_inverse, s, basis, occ, left_order, down_order, numbers, coarse_inverse):
    r, s_inverse, s, basis = r[:, 0], s_inverse[:, 0], s[:, 0], basis[:, 0]
    place = jnp.stack([lax.axis_index(BLK), lax.axis_index("xh"), lax.axis_index(NEAR)]).astype(jnp.int32)
    operand = pltpu.VMEM((2, 4 * F, R), BF16)
    strip = pltpu.VMEM((F, 4 * F), BF16)

    right, up = call(pack_kernel, [((2, PACK, R), F32), ((PACK, R), F32)], r, occ, basis)
    r_left = moved(right, CROSS, 32, 1)
    r_down = moved(up, BLK, 8, 1)
    (loads,) = call(loads_kernel, [((16, 8, R), F32)], r, basis)
    far = lax.all_to_all(loads, FAR, 0, 0)
    first_block, later_block = call(
        coarse_block_kernel,
        [((16 * SLOTS, 16 * 8), F32), ((16 * SLOTS, 16 * SLOTS), F32)],
        place, numbers[None, :], coarse_inverse,
        smem=(0,), near_out=(0, 1),
    )
    schur_block, schur_here = call(
        reorder_weighted_kernel,
        [(s.shape, BF16), (s.shape, BF16)],
        s, left_order, down_order, occ,
        flops=2 * MATMUL_FLOPS, near_out=(1,), scratch=[strip],
    )
    r_left, r_down, first_block, later_block, schur_here = lax.optimization_barrier(
        (r_left, r_down, first_block, later_block, schur_here)
    )

    halves = call(
        first_kernel, HALVES, r, r_left, r_down, schur_here,
        flops=MATMUL_FLOPS, near=(1, 2, 3), scratch=[operand],
    )
    far, s_inverse, *halves = lax.optimization_barrier((far, s_inverse, *halves))
    others = exchanged(*halves[:4])
    (partial,) = call(partial_kernel, [((16, SLOTS, R), F32)], far, first_block, near=(0, 1))
    values = lax.all_to_all(partial, NEAR, 0, 0)
    (inverse_block,) = call(
        reorder_plain_kernel,
        [(s_inverse.shape, BF16)],
        s_inverse, left_order, down_order,
        flops=2 * MATMUL_FLOPS, scratch=[strip],
    )
    rows, columns = call(
        basis_kernel,
        [((FACES, 48, F), BF16), ((FACES, F, 128), BF16)],
        basis, r_left, r_down,
        scratch=[pltpu.VMEM((SLOTS, F), F32)],
    )
    z0, *halves, message, corners = call(
        operate_first_kernel,
        [((FACES, F, R), F32), *HALVES, ((16, SLOTS, R), F32), ((SLOTS, R), F32)],
        values, columns, *halves, *others, r, rows, inverse_block,
        flops=MATMUL_FLOPS, near=(0, 7, 8, 9, 10), scratch=[operand],
    )
    others = exchanged(*halves[:4])
    far = lax.all_to_all(message, FAR, 0, 0)
    (partial,) = call(partial_kernel, [((16, SLOTS, R), F32)], far, later_block, near=(0, 1))
    values = lax.all_to_all(partial, NEAR, 0, 0)
    residual, image, *halves, corners, scalars = call(
        second_kernel,
        [((4, F, R), F32), ((4, F, R), F32), *HALVES, ((SLOTS, R), F32), ((8, R), F32)],
        values, corners, r_left, r_down, r, *halves, *others, schur_block,
        flops=MATMUL_FLOPS, near=(0, 10, 11, 12, 13), near_out=(0, 1, 2, 3, 4, 5, 6, 7), scratch=[operand],
    )
    others = exchanged(*halves[:4])
    z1, message = call(
        operate_last_kernel,
        [((4, F, R), F32), ((16, 4, R), F32)],
        corners, columns, *halves, *others, residual, image, inverse_block, z0,
        flops=MATMUL_FLOPS, near=tuple(range(15)), near_out=(0,), scratch=[operand, pltpu.VMEM((FACES, F, R), F32)],
    )
    near = lax.all_to_all(message, NEAR, 0, 0)
    (spread_sums,) = call(sum_kernel, [((16, 4, R), F32)], near, near=(0,))
    sums = lax.all_to_all(spread_sums, FAR, 0, 0)
    (out,) = call(finish_kernel, [((2, 2 * F, R), F32)], sums, scalars, z0, z1, near=(0, 1, 2, 3))
    return out[:, None]


def solution(mesh):
    split = Mesh(mesh.devices.reshape(tuple(SPLIT.values())), tuple(SPLIT))
    four = P(BLK, CROSS, None, None)
    three = P(BLK, CROSS, None)
    return jax.shard_map(
        on_device,
        mesh=split,
        in_specs=(four, four, four, four, three, three, three, P(), P()),
        out_specs=four,
        check_vma=False,
    )
```

```python
import jax
import jax.numpy as jnp
from jax import lax
from jax.experimental import pallas as pl
from jax.experimental.pallas import tpu as pltpu
from jax.sharding import Mesh
from jax.sharding import PartitionSpec as P

SPLIT = {"y": 4, "xl": 2, "xh": 2, "z": 8, "c": 2}
BLK = ("y", "xl")
CROSS = ("xh", "z", "c")
NEAR = ("z", "c")
FAR = ("y", "xl", "xh")
F = 256
R = 256
CORNERS = 512
EXACT = lax.Precision.HIGHEST
F32 = jnp.float32
BF16 = jnp.bfloat16

FACES = 7
PACK = F + 8
WEIGHT = F + 4
SIDES = ((4, 0, 6, 2), (5, 1, 2, 3))
OWNER = ((0, 0), (1, 0), (0, 0), (1, 0), (0, -1), (1, -1), (-1, 0))


def slot(axial, sector):
    return (axial + 1) * 3 + sector + 1


SLOTS = 16


def face_slots(face):
    axial, sector = OWNER[face]
    return [slot(axial + da, sector + ds) for da in (0, 1) for ds in (0, 1)]


class Fetched:
    def __init__(self, source, held, sems, pieces):
        self.held = held
        self.copies = {
            str(piece): pltpu.make_async_copy(source.at[piece], held.at[piece], sem)
            for piece, sem in zip(pieces, sems)
        }
        self.waited = set()

    def start(self):
        for copy in self.copies.values():
            copy.start()

    def get(self, piece=()):
        if str(piece) not in self.waited:
            self.waited.add(str(piece))
            self.copies[str(piece)].wait()
        return self.held.at[piece] if piece else self.held

    def finish(self):
        for piece, copy in self.copies.items():
            if piece not in self.waited:
                copy.wait()


class Stored:
    def __init__(self, held, target, sems, pieces):
        self.held = held
        self.copies = {
            str(piece): pltpu.make_async_copy(held.at[piece], target.at[piece], sem)
            for piece, sem in zip(pieces, sems)
        }

    def put(self, value, piece=()):
        self.held[piece if piece else ...] = value
        self.copies[str(piece)].start()

    def send(self, piece=()):
        self.copies[str(piece)].start()

    def finish(self):
        for copy in self.copies.values():
            copy.wait()


BLOCK_PIECES = [(k, slice(side * F, (side + 1) * F)) for k in range(2) for side in range(4)]


HALF_PIECES = [(k, slice(side * F, (side + 1) * F)) for k in range(2) for side in range(2)]


def pieces_of(shape):
    if shape == (2, 4 * F, 4 * F):
        return BLOCK_PIECES
    if shape == (2, 2 * F, R):
        return HALF_PIECES
    if len(shape) == 3 and shape[1:] in ((F, R), (PACK, R)):
        return [(k,) for k in range(shape[0])]
    return [()]


def block_piece(k, side):
    return BLOCK_PIECES[k * 4 + side]


class Here:
    def __init__(self, held):
        self.held = held

    def start(self):
        pass

    def get(self, piece=()):
        return self.held.at[piece] if piece else self.held

    def put(self, value, piece=()):
        self.held[piece if piece else ...] = value

    def send(self, piece=()):
        pass

    def finish(self):
        pass


def call(kernel, outs, *args, smem=(), near=(), near_out=(), parts=None, scratch=()):
    inputs = [i for i in range(len(args)) if i not in smem]
    shapes = [(args[i].shape, args[i].dtype) for i in inputs] + list(outs)
    here = [i in near for i in inputs] + [i in near_out for i in range(len(outs))]
    pieces = [[] if there else pieces_of(shape) for (shape, _), there in zip(shapes, here)]
    for i, count in (parts or {}).items():
        pieces[i] = pieces[i][:count]
    staged = [shape for shape, there in zip(shapes, here) if not there]

    def body(*refs):
        operands, results = refs[: len(args)], refs[len(args) : len(args) + len(outs)]
        rest = list(refs[len(args) + len(outs) :])
        held, sems, rest = rest[: len(staged)], rest[len(staged)], rest[len(staged) + 1 :]
        made, at = [], 0
        for i, (ref, there) in enumerate(zip([operands[i] for i in inputs] + list(results), here)):
            if there:
                made.append(Here(ref))
                continue
            own = [sems.at[at + j] for j in range(len(pieces[i]))]
            at += len(own)
            vmem = held.pop(0)
            fetch = i < len(inputs)
            made.append(Fetched(ref, vmem, own, pieces[i]) if fetch else Stored(vmem, ref, own, pieces[i]))
        for operand in made[: len(inputs)]:
            operand.start()
        kernel(*[operands[i] for i in smem], *made, *rest)
        for array in made:
            array.finish()

    args = [a if i in smem or i in near else pltpu.with_memory_space_constraint(a, pltpu.HBM) for i, a in enumerate(args)]

    def space(there):
        return pl.BlockSpec(memory_space=pltpu.VMEM if there else pltpu.HBM)

    return pl.pallas_call(
        body,
        out_shape=[
            jax.ShapeDtypeStruct(s, d) if i in near_out else pltpu.HBM(s, d) for i, (s, d) in enumerate(outs)
        ],
        in_specs=[pl.BlockSpec(memory_space=pltpu.SMEM) if i in smem else space(i in near) for i in range(len(args))],
        out_specs=[space(i in near_out) for i in range(len(outs))],
        scratch_shapes=[pltpu.VMEM(s, d) for s, d in staged]
        + [pltpu.SemaphoreType.DMA((max(1, sum(len(p) for p in pieces)),)), *scratch],
        compiler_params=pltpu.CompilerParams(vmem_limit_bytes=32 * 1024 * 1024),
        cost_estimate=pl.CostEstimate(flops=0, bytes_accessed=0, transcendentals=0),
    )(*args)


def thirds(value):
    high = value.astype(BF16)
    rest = value - high.astype(F32)
    middle = rest.astype(BF16)
    return high, middle, (rest - middle.astype(F32)).astype(BF16)


def nt(left, right):
    return lax.dot_general(left, right, (((1,), (1,)), ((), ())), preferred_element_type=F32)


def nn(left, right):
    return lax.dot_general(left, right, (((1,), (0,)), ((), ())), preferred_element_type=F32)


def weights_of(occ_ref, k):
    return 1.0 / (1.0 + occ_ref[k].astype(F32))


def open_kernel(r, occ, basis, right, up, loads):
    basis_ref, occ_ref = basis.get(), occ.get()

    def tail(k, part):
        spare = jnp.zeros((3, R), F32)
        return jnp.concatenate([basis_ref[k, :, part], weights_of(occ_ref, k)[:, part], spare], axis=0)

    first, last = slice(0, F), slice(F, 2 * F)
    right.held[0, F:, :] = tail(0, first)
    right.held[1, F:, :] = tail(1, first)
    up.held[F:, :] = tail(1, last)
    for k in range(2):
        right.held[k, :F, :] = own_face(r, k)
        right.send((k,))
    up.held[:F, :] = own_face(r, 3)
    up.send()
    own_face(r, 2)
    one = jnp.dot(basis_ref[0], r.held[0], precision=EXACT, preferred_element_type=F32)
    two = jnp.dot(basis_ref[1], r.held[1], precision=EXACT, preferred_element_type=F32)
    rows = jnp.concatenate([one[0:2], one[2:4] + two[0:2], two[2:4], jnp.zeros((2, R), F32)], axis=0)
    for peer in range(16):
        loads.held[peer] = rows
    loads.send()


def scale_column(row):
    eye = lax.broadcasted_iota(jnp.int32, (F, F), 1) == lax.broadcasted_iota(jnp.int32, (F, F), 0)
    return jnp.sum(jnp.where(eye, row, 0.0), axis=1, keepdims=True)


def placed(order_row):
    rows = lax.broadcasted_iota(jnp.int32, (F, F), 0)
    return jnp.where(order_row == rows, -1.0, 0.0).astype(BF16)


def reorder_block(s, outs, work_ref, k, orders, weights):
    for row in range(4):
        rows = s.get(block_piece(k, row))
        for side in range(4):
            part = rows[:, side * F : (side + 1) * F]
            if orders[side] is not None:
                part = nt(part, orders[side])
            if weights[side] is not None:
                part = part.astype(F32) * weights[side]
            work_ref[:, side * F : (side + 1) * F] = part.astype(BF16)
        part = work_ref[...]
        if orders[row] is not None:
            part = nn(orders[row], part)
        if weights[row] is not None:
            part = part.astype(F32) * scale_column(weights[row])
        for out in outs:
            out.put(part.astype(BF16), block_piece(k, row))


def reorder_plain_kernel(s, left, down, out, work_ref):
    left_ref, down_ref = left.get(), down.get()
    for k in range(2):
        orders = (placed(left_ref[k]), None, placed(down_ref[k]), None)
        reorder_block(s, (out,), work_ref, k, orders, (None,) * 4)


def reorder_weighted_kernel(s, left, down, occ, out, twin, work_ref):
    left_ref, down_ref, occ_ref = left.get(), down.get(), occ.get()
    first, second = weights_of(occ_ref, 0), weights_of(occ_ref, 1)
    for k, weight in enumerate((first, second)):
        orders = (placed(left_ref[k]), None, placed(down_ref[k]), None)
        below = None if k == 0 else first[:, F:]
        reorder_block(s, (out, twin), work_ref, k, orders, (None, weight[:, :F], below, weight[:, F:]))


def basis_kernel(basis, from_left, from_down, rows, columns, flat_ref):
    basis_ref, from_down_ref = basis.get(), from_down.get()
    sources = (
        basis_ref[0, :, :F],
        basis_ref[1, :, :F],
        basis_ref[0, :, F:],
        basis_ref[1, :, F:],
        from_left.get((0,))[F : F + 4, :],
        from_left.get((1,))[F : F + 4, :],
        from_down_ref[F : F + 4, :],
    )
    for face in range(FACES):
        flat_ref[...] = jnp.zeros_like(flat_ref)
        for k, row in enumerate(face_slots(face)):
            flat_ref[row : row + 1, :] = sources[face][k : k + 1, :]
        high, middle, low = thirds(flat_ref[...])
        rows.held[face, 0:16, :] = high
        rows.held[face, 16:32, :] = middle
        rows.held[face, 32:48, :] = low
        parts = [p.astype(F32) for p in (high, high, high, middle, middle, low)]
        parts.append(jnp.zeros((32, F), F32))
        columns.held[face] = jnp.concatenate(parts, axis=0).T.astype(BF16)
    rows.send()
    columns.send()


def corner_onehot(numbers_t, axial, sector, spare):
    wanted = (axial & 15) * 32 + (sector & 31)
    columns = lax.broadcasted_iota(jnp.int32, (wanted.shape[0], CORNERS), 1)
    picks = jnp.where((columns == wanted) & jnp.logical_not(spare), 1.0, 0.0).astype(BF16)
    return nt(picks, numbers_t).astype(BF16)


def coarse_block_kernel(place_ref, numbers, inverse, first, later):
    blk, xh, near = place_ref[0], place_ref[1], place_ref[2]
    ids = lax.broadcasted_iota(jnp.int32, (CORNERS, CORNERS), 0)
    numbers_t = jnp.where(numbers.get()[...] == ids, 1.0, 0.0).astype(BF16)
    rows = lax.broadcasted_iota(jnp.int32, (16 * SLOTS, 1), 0)
    peer = rows >> 4
    entry = rows & 15
    third = (entry >= 3).astype(jnp.int32) + (entry >= 6).astype(jnp.int32) + (entry >= 9).astype(jnp.int32)
    da = third - 1
    ds = entry - 3 * third - 1
    spare = entry >= 12
    far_rows = corner_onehot(numbers_t, 2 * (peer >> 1) + da, (peer & 1) * 16 + near + ds, spare)
    near_rows = corner_onehot(numbers_t, 2 * blk + da, xh * 16 + peer + ds, spare)
    few = lax.broadcasted_iota(jnp.int32, (16 * 8, 1), 0)
    source, own = few >> 3, few & 7
    own_rows = corner_onehot(
        numbers_t, 2 * (source >> 1) + (own >> 1), (source & 1) * 16 + near + (own & 1), own >= 6
    )
    terms = thirds(inverse.get()[...])[::-1]
    picked = thirds(sum(nn(near_rows, part) for part in terms))[::-1]
    first.put(sum(nt(part, own_rows) for part in picked))
    block = sum(nt(part, far_rows) for part in picked).T
    columns = lax.broadcasted_iota(jnp.int32, (16 * SLOTS, 16 * SLOTS), 1) & 15
    passed = (columns == entry) & spare
    later.put(jnp.where(passed, 1.0, block))


HALVES = [((2, F, R), F32), ((2, F, R), F32), ((F, R), F32), ((F, R), F32), ((F, R), F32)]


def apply_block(s, operand_ref, left, right, up, down, mid, weights=None, seen=None):
    stores = {
        0: lambda v: right.put(v, (0,)),
        1: lambda v: right.put(v, (1,)),
        2: mid.put,
        3: up.put,
        4: lambda v: left.put(v, (0,)),
        5: lambda v: left.put(v, (1,)),
        6: down.put,
    }
    shared = None
    for k in range(2):
        for side in range(4):
            face = SIDES[k][side]
            image = nn(s.get(block_piece(k, side))[...], operand_ref[k])
            if face == 2:
                if shared is None:
                    shared = image
                    continue
                image = shared + image
            if weights is not None and face >= 4:
                image = image * weights[face - 4]
            stores[face](image)
            if seen is not None:
                seen(face, image)


def set_operand(operand_ref, face, value):
    value = value.astype(BF16)
    for k in range(2):
        for side in range(4):
            if SIDES[k][side] == face:
                operand_ref[k, side * F : (side + 1) * F, :] = value


def outer_weights(from_left, from_down):
    rows = [from_left.get((k,))[WEIGHT : WEIGHT + 1, :] for k in range(2)]
    rows.append(from_down.get()[WEIGHT : WEIGHT + 1, :])
    return [scale_column(row) for row in rows]


def first_kernel(r, from_left, from_down, s, left, right, up, down, mid, operand_ref):
    weights = outer_weights(from_left, from_down)
    set_operand(operand_ref, 6, from_down.get()[:F, :] * weights[2])
    for k in range(2):
        set_operand(operand_ref, 4 + k, from_left.get((k,))[:F, :] * weights[k])
    for face in range(4):
        set_operand(operand_ref, face, own_face(r, face))
    apply_block(s, operand_ref, left, right, up, down, mid, weights)


PLACES = ((1, (0,)), (1, (1,)), (4, ()), (2, ()), (0, (0,)), (0, (1,)), (3, ()))


def own_share(halves, face):
    which, piece = PLACES[face]
    return halves[which].get(piece)[...]


def assembled(halves, others, face):
    which, piece = PLACES[face]
    if which == 4:
        return own_share(halves, face)
    return own_share(halves, face) + others[which].get(piece)[...]


def stacked(values):
    high, middle, low = thirds(values)
    parts = [high, middle, low, high, middle, high, jnp.zeros((32, R), BF16)]
    return jnp.concatenate(parts, axis=0)


def face_loads(rows_ref, face, image):
    out = sum(nn(rows_ref[face], part) for part in thirds(image)[1::-1])
    return out[32:48] + out[16:32] + out[0:16]


def face_piece(face):
    return HALF_PIECES[(face % 2) * 2 + face // 2]


def own_face(r, face):
    return r.get(face_piece(face))[...]


def total(value):
    return jnp.sum(value, axis=0, keepdims=True)


def operate_first_kernel(
    values, columns, l0, r0, u0, d0, m0, fl, fr, fu, fd, r, rows, s,
    z, left, right, up, down, mid, message, corners_out, operand_ref,
):
    corners = jnp.sum(values.get()[...], axis=0)
    corners_out.put(corners)
    terms = stacked(corners)
    columns_ref = columns.get()
    before, others = (l0, r0, u0, d0, m0), (fl, fr, fu, fd)
    images = (left, right, up, down, mid)
    progress = jnp.zeros((1, R), F32)
    for face in range(FACES):
        value = assembled(before, others, face) + nn(columns_ref[face], terms)
        z.put(value, (face,))
        set_operand(operand_ref, face, value)
        if face < 4:
            progress = progress + total(own_face(r, face) * value)
    rows_ref = rows.get()
    sums = [jnp.zeros((SLOTS, R), F32), jnp.zeros((1, R), F32)]

    def seen(face, image):
        sums[0] = sums[0] + face_loads(rows_ref, face, image)
        sums[1] = sums[1] + total(z.held[face] * image)

    apply_block(s, operand_ref, *images, seen=seen)
    loads, curvature = sums
    for peer in range(16):
        message.held[peer] = loads
        message.held[peer, 12:13, :] = progress
        message.held[peer, 13:14, :] = curvature
    message.send()


def second_kernel(
    values, corners_before, r_left, r_down, r, l0, r0, u0, d0, m0, fl, fr, fu, fd, s,
    residual, image_out, left, right, up, down, mid, corners_out, scalars, operand_ref,
):
    sums = jnp.sum(values.get()[...], axis=0)
    progress, curvature = sums[12:13, :], sums[13:14, :]
    alpha = progress / curvature
    corners_out.put(corners_before.get()[...] - alpha * sums)
    scalars.held[...] = jnp.zeros((8, R), F32)
    scalars.held[0:1, :] = progress
    scalars.held[1:2, :] = curvature
    scalars.held[2:3, :] = alpha
    scalars.send()
    before, others = (l0, r0, u0, d0, m0), (fl, fr, fu, fd)
    weights = outer_weights(r_left, r_down)
    for face in range(FACES):
        image = assembled(before, others, face)
        if face < 4:
            start = own_face(r, face)
        elif face < 6:
            start = r_left.get((face - 4,))[:F, :]
        else:
            start = r_down.get()[:F, :]
        value = start - alpha * image
        if face < 4:
            image_out.put(image, (face,))
            residual.put(value, (face,))
        else:
            value = value * weights[face - 4]
        set_operand(operand_ref, face, value)
    apply_block(s, operand_ref, left, right, up, down, mid, weights)


def operate_last_kernel(
    corners_in, columns, l0, r0, u0, d0, m0, fl, fr, fu, fd, residual, image_in, s, z0,
    z, message, operand_ref, z_ref,
):
    corners = corners_in.get()[...]
    terms = stacked(jnp.where(lax.broadcasted_iota(jnp.int32, corners.shape, 0) < 12, corners, 0.0))
    columns_ref = columns.get()
    before, others = (l0, r0, u0, d0, m0), (fl, fr, fu, fd)
    progress = jnp.zeros((1, R), F32)
    mixed = jnp.zeros((1, R), F32)
    for face in range(FACES):
        value = assembled(before, others, face) + nn(columns_ref[face], terms)
        z_ref[face] = value
        set_operand(operand_ref, face, value)
        if face < 4:
            z.put(value, (face,))
            progress = progress + total(residual.get((face,))[...] * value)
            mixed = mixed + total(image_in.get((face,))[...] * value)
    curvature = jnp.zeros((1, R), F32)
    for k in range(2):
        for side in range(4):
            image = nn(s.get(block_piece(k, side))[...], operand_ref[k])
            face = SIDES[k][side]
            curvature = curvature + total(z_ref[face] * image)
            mixed = mixed + total(z0.get((face,))[...] * image)
    for peer in range(16):
        message.held[peer, 0:1, :] = progress
        message.held[peer, 1:2, :] = curvature
        message.held[peer, 2:3, :] = mixed
        message.held[peer, 3:4, :] = jnp.zeros((1, R), F32)
    message.send()


def finish_kernel(sums_in, scalars, z0, z1, out):
    sums = jnp.sum(sums_in.get()[...], axis=0)
    progress, curvature, mixed = sums[0:1, :], sums[1:2, :], sums[2:3, :]
    before = scalars.get()[...]
    first_progress, first_curvature, alpha = before[0:1, :], before[1:2, :], before[2:3, :]
    ratio = progress / first_progress
    last = progress / (curvature + ratio * (mixed + ratio * first_curvature))
    scale0 = alpha + last * ratio
    for face in (0, 2, 1, 3):
        out.put(scale0 * z0.get((face,))[...] + last * z1.get((face,))[...], face_piece(face))


def partial_kernel(message, block, out):
    flat = jnp.concatenate([message.get()[i] for i in range(16)], axis=0)
    values = jnp.dot(block.get()[...], flat, precision=EXACT, preferred_element_type=F32)
    for i in range(16):
        out.held[i] = values[i * SLOTS : (i + 1) * SLOTS]
    out.send()


def sum_kernel(near, out):
    sums = jnp.sum(near.get()[...], axis=0)
    for i in range(16):
        out.held[i] = sums
    out.send()


def moved(block, axes, count, distance):
    return lax.ppermute(block, axes, [(i, (i + distance) % count) for i in range(count)])


def exchanged(left, right, up, down):
    return (
        moved(right, CROSS, 32, 1),
        moved(left, CROSS, 32, -1),
        moved(down, BLK, 8, -1),
        moved(up, BLK, 8, 1),
    )


def on_device(r, s_inverse, s, basis, occ, left_order, down_order, numbers, coarse_inverse):
    r, s_inverse, s, basis = r[:, 0], s_inverse[:, 0], s[:, 0], basis[:, 0]
    place = jnp.stack([lax.axis_index(BLK), lax.axis_index("xh"), lax.axis_index(NEAR)]).astype(jnp.int32)
    operand = pltpu.VMEM((2, 4 * F, R), BF16)
    strip = pltpu.VMEM((F, 4 * F), BF16)

    right, up, loads = call(
        open_kernel, [((2, PACK, R), F32), ((PACK, R), F32), ((16, 8, R), F32)], r, occ, basis
    )
    r_left = moved(right, CROSS, 32, 1)
    r_down = moved(up, BLK, 8, 1)
    far = lax.all_to_all(loads, FAR, 0, 0)
    first_block, later_block = call(
        coarse_block_kernel,
        [((16 * SLOTS, 16 * 8), F32), ((16 * SLOTS, 16 * SLOTS), F32)],
        place, numbers[None, :], coarse_inverse,
        smem=(0,), near_out=(0, 1),
    )
    schur_block, schur_here = call(
        reorder_weighted_kernel,
        [(s.shape, BF16), (s.shape, BF16)],
        s, left_order, down_order, occ,
        near_out=(1,), scratch=[strip],
    )
    r_left, r_down, first_block, later_block, schur_here = lax.optimization_barrier(
        (r_left, r_down, first_block, later_block, schur_here)
    )

    halves = call(
        first_kernel, HALVES, r, r_left, r_down, schur_here,
        near=(1, 2, 3), scratch=[operand],
    )
    far, s_inverse, *halves = lax.optimization_barrier((far, s_inverse, *halves))
    others = exchanged(*halves[:4])
    (partial,) = call(partial_kernel, [((16, SLOTS, R), F32)], far, first_block, near=(0, 1))
    values = lax.all_to_all(partial, NEAR, 0, 0)
    (inverse_block,) = call(
        reorder_plain_kernel,
        [(s_inverse.shape, BF16)],
        s_inverse, left_order, down_order,
        scratch=[strip],
    )
    rows, columns = call(
        basis_kernel,
        [((FACES, 48, F), BF16), ((FACES, F, 128), BF16)],
        basis, r_left, r_down,
        scratch=[pltpu.VMEM((SLOTS, F), F32)],
    )
    z0, *halves, message, corners = call(
        operate_first_kernel,
        [((FACES, F, R), F32), *HALVES, ((16, SLOTS, R), F32), ((SLOTS, R), F32)],
        values, columns, *halves, *others, r, rows, inverse_block,
        near=(0, 7, 8, 9, 10), scratch=[operand],
    )
    others = exchanged(*halves[:4])
    near = lax.all_to_all(message, NEAR, 0, 0)
    (partial,) = call(partial_kernel, [((16, SLOTS, R), F32)], near, later_block, near=(0, 1))
    values = lax.all_to_all(partial, FAR, 0, 0)
    residual, image, *halves, corners, scalars = call(
        second_kernel,
        [((4, F, R), F32), ((4, F, R), F32), *HALVES, ((SLOTS, R), F32), ((8, R), F32)],
        values, corners, r_left, r_down, r, *halves, *others, schur_block,
        near=(0, 10, 11, 12, 13), near_out=(0, 1, 2, 3, 4, 5, 6, 7), scratch=[operand],
    )
    others = exchanged(*halves[:4])
    z1, message = call(
        operate_last_kernel,
        [((4, F, R), F32), ((16, 4, R), F32)],
        corners, columns, *halves, *others, residual, image, inverse_block, z0,
        near=tuple(range(15)), near_out=(0,), scratch=[operand, pltpu.VMEM((FACES, F, R), F32)],
    )
    near = lax.all_to_all(message, NEAR, 0, 0)
    (spread_sums,) = call(sum_kernel, [((16, 4, R), F32)], near, near=(0,))
    sums = lax.all_to_all(spread_sums, FAR, 0, 0)
    (out,) = call(finish_kernel, [((2, 2 * F, R), F32)], sums, scalars, z0, z1, near=(0, 1, 2, 3))
    return out[:, None]


def solution(mesh):
    split = Mesh(mesh.devices.reshape(tuple(SPLIT.values())), tuple(SPLIT))
    four = P(BLK, CROSS, None, None)
    three = P(BLK, CROSS, None)
    return jax.shard_map(
        on_device,
        mesh=split,
        in_specs=(four, four, four, four, three, three, three, P(), P()),
        out_specs=four,
        check_vma=False,
    )
```

```python
import jax
import jax.numpy as jnp
from jax import lax
from jax.experimental import pallas as pl
from jax.experimental.pallas import tpu as pltpu
from jax.sharding import Mesh
from jax.sharding import PartitionSpec as P

SPLIT = {"y": 4, "xl": 2, "xh": 2, "z": 8, "c": 2}
BLK = ("y", "xl")
CROSS = ("xh", "z", "c")
NEAR = ("z", "c")
FAR = ("y", "xl", "xh")
F = 256
R = 256
CORNERS = 512
EXACT = lax.Precision.HIGHEST
F32 = jnp.float32
BF16 = jnp.bfloat16

FACES = 7
PACK = F + 8
WEIGHT = F + 4
SIDES = ((4, 0, 6, 2), (5, 1, 2, 3))
OWNER = ((0, 0), (1, 0), (0, 0), (1, 0), (0, -1), (1, -1), (-1, 0))


def slot(axial, sector):
    return (axial + 1) * 3 + sector + 1


SLOTS = 16


def face_slots(face):
    axial, sector = OWNER[face]
    return [slot(axial + da, sector + ds) for da in (0, 1) for ds in (0, 1)]


class Fetched:
    def __init__(self, source, held, sems, pieces):
        self.held = held
        self.copies = {
            str(piece): pltpu.make_async_copy(source.at[piece], held.at[piece], sem)
            for piece, sem in zip(pieces, sems)
        }
        self.waited = set()

    def start(self):
        for copy in self.copies.values():
            copy.start()

    def get(self, piece=()):
        if str(piece) not in self.waited:
            self.waited.add(str(piece))
            self.copies[str(piece)].wait()
        return self.held.at[piece] if piece else self.held

    def finish(self):
        for piece, copy in self.copies.items():
            if piece not in self.waited:
                copy.wait()


class Stored:
    def __init__(self, held, target, sems, pieces):
        self.held = held
        self.copies = {
            str(piece): pltpu.make_async_copy(held.at[piece], target.at[piece], sem)
            for piece, sem in zip(pieces, sems)
        }

    def put(self, value, piece=()):
        self.held[piece if piece else ...] = value
        self.copies[str(piece)].start()

    def send(self, piece=()):
        self.copies[str(piece)].start()

    def finish(self):
        for copy in self.copies.values():
            copy.wait()


BLOCK_PIECES = [(k, slice(side * F, (side + 1) * F)) for k in range(2) for side in range(4)]


HALF_PIECES = [(k, slice(side * F, (side + 1) * F)) for k in range(2) for side in range(2)]


def pieces_of(shape):
    if shape == (2, 4 * F, 4 * F):
        return BLOCK_PIECES
    if shape == (2, 2 * F, R):
        return HALF_PIECES
    if len(shape) == 3 and shape[1:] in ((F, R), (PACK, R)):
        return [(k,) for k in range(shape[0])]
    return [()]


def block_piece(k, side):
    return BLOCK_PIECES[k * 4 + side]


class Here:
    def __init__(self, held):
        self.held = held

    def start(self):
        pass

    def get(self, piece=()):
        return self.held.at[piece] if piece else self.held

    def put(self, value, piece=()):
        self.held[piece if piece else ...] = value

    def send(self, piece=()):
        pass

    def finish(self):
        pass


def call(kernel, outs, *args, smem=(), near=(), near_out=(), parts=None, scratch=()):
    inputs = [i for i in range(len(args)) if i not in smem]
    shapes = [(args[i].shape, args[i].dtype) for i in inputs] + list(outs)
    here = [i in near for i in inputs] + [i in near_out for i in range(len(outs))]
    pieces = [[] if there else pieces_of(shape) for (shape, _), there in zip(shapes, here)]
    for i, count in (parts or {}).items():
        pieces[i] = pieces[i][:count]
    staged = [shape for shape, there in zip(shapes, here) if not there]

    def body(*refs):
        operands, results = refs[: len(args)], refs[len(args) : len(args) + len(outs)]
        rest = list(refs[len(args) + len(outs) :])
        held, sems, rest = rest[: len(staged)], rest[len(staged)], rest[len(staged) + 1 :]
        made, at = [], 0
        for i, (ref, there) in enumerate(zip([operands[i] for i in inputs] + list(results), here)):
            if there:
                made.append(Here(ref))
                continue
            own = [sems.at[at + j] for j in range(len(pieces[i]))]
            at += len(own)
            vmem = held.pop(0)
            fetch = i < len(inputs)
            made.append(Fetched(ref, vmem, own, pieces[i]) if fetch else Stored(vmem, ref, own, pieces[i]))
        for operand in made[: len(inputs)]:
            operand.start()
        kernel(*[operands[i] for i in smem], *made, *rest)
        for array in made:
            array.finish()

    args = [a if i in smem or i in near else pltpu.with_memory_space_constraint(a, pltpu.HBM) for i, a in enumerate(args)]

    def space(there):
        return pl.BlockSpec(memory_space=pltpu.VMEM if there else pltpu.HBM)

    return pl.pallas_call(
        body,
        out_shape=[
            jax.ShapeDtypeStruct(s, d) if i in near_out else pltpu.HBM(s, d) for i, (s, d) in enumerate(outs)
        ],
        in_specs=[pl.BlockSpec(memory_space=pltpu.SMEM) if i in smem else space(i in near) for i in range(len(args))],
        out_specs=[space(i in near_out) for i in range(len(outs))],
        scratch_shapes=[pltpu.VMEM(s, d) for s, d in staged]
        + [pltpu.SemaphoreType.DMA((max(1, sum(len(p) for p in pieces)),)), *scratch],
        compiler_params=pltpu.CompilerParams(vmem_limit_bytes=32 * 1024 * 1024),
        cost_estimate=pl.CostEstimate(flops=0, bytes_accessed=0, transcendentals=0),
    )(*args)


def thirds(value):
    high = value.astype(BF16)
    rest = value - high.astype(F32)
    middle = rest.astype(BF16)
    return high, middle, (rest - middle.astype(F32)).astype(BF16)


def nt(left, right):
    return lax.dot_general(left, right, (((1,), (1,)), ((), ())), preferred_element_type=F32)


def nn(left, right):
    return lax.dot_general(left, right, (((1,), (0,)), ((), ())), preferred_element_type=F32)


def weights_of(occ_ref, k):
    return 1.0 / (1.0 + occ_ref[k].astype(F32))


def open_kernel(r, occ, basis, right, up, loads):
    basis_ref, occ_ref = basis.get(), occ.get()

    def tail(k, part):
        spare = jnp.zeros((3, R), F32)
        return jnp.concatenate([basis_ref[k, :, part], weights_of(occ_ref, k)[:, part], spare], axis=0)

    first, last = slice(0, F), slice(F, 2 * F)
    right.held[0, F:, :] = tail(0, first)
    right.held[1, F:, :] = tail(1, first)
    up.held[F:, :] = tail(1, last)
    for k in range(2):
        right.held[k, :F, :] = own_face(r, k)
        right.send((k,))
    up.held[:F, :] = own_face(r, 3)
    up.send()
    own_face(r, 2)
    one = jnp.dot(basis_ref[0], r.held[0], precision=EXACT, preferred_element_type=F32)
    two = jnp.dot(basis_ref[1], r.held[1], precision=EXACT, preferred_element_type=F32)
    rows = jnp.concatenate([one[0:2], one[2:4] + two[0:2], two[2:4], jnp.zeros((2, R), F32)], axis=0)
    for peer in range(16):
        loads.held[peer] = rows
    loads.send()


def scale_column(row):
    eye = lax.broadcasted_iota(jnp.int32, (F, F), 1) == lax.broadcasted_iota(jnp.int32, (F, F), 0)
    return jnp.sum(jnp.where(eye, row, 0.0), axis=1, keepdims=True)


def placed(order_row):
    rows = lax.broadcasted_iota(jnp.int32, (F, F), 0)
    return jnp.where(order_row == rows, -1.0, 0.0).astype(BF16)


def reorder_block(s, outs, work_ref, k, orders, weights):
    for row in range(4):
        rows = s.get(block_piece(k, row))
        for side in range(4):
            part = rows[:, side * F : (side + 1) * F]
            if orders[side] is not None:
                part = nt(part, orders[side])
            if weights[side] is not None:
                part = part.astype(F32) * weights[side]
            work_ref[:, side * F : (side + 1) * F] = part.astype(BF16)
        part = work_ref[...]
        if orders[row] is not None:
            part = nn(orders[row], part)
        if weights[row] is not None:
            part = part.astype(F32) * scale_column(weights[row])
        for out in outs:
            out.put(part.astype(BF16), block_piece(k, row))


def reorder_plain_kernel(s, left, down, out, work_ref):
    left_ref, down_ref = left.get(), down.get()
    for k in range(2):
        orders = (placed(left_ref[k]), None, placed(down_ref[k]), None)
        reorder_block(s, (out,), work_ref, k, orders, (None,) * 4)


def reorder_weighted_kernel(s, left, down, occ, out, twin, work_ref):
    left_ref, down_ref, occ_ref = left.get(), down.get(), occ.get()
    first, second = weights_of(occ_ref, 0), weights_of(occ_ref, 1)
    for k, weight in enumerate((first, second)):
        orders = (placed(left_ref[k]), None, placed(down_ref[k]), None)
        below = None if k == 0 else first[:, F:]
        reorder_block(s, (out, twin), work_ref, k, orders, (None, weight[:, :F], below, weight[:, F:]))


def basis_kernel(basis, from_left, from_down, rows, columns, flat_ref):
    basis_ref, from_down_ref = basis.get(), from_down.get()
    sources = (
        basis_ref[0, :, :F],
        basis_ref[1, :, :F],
        basis_ref[0, :, F:],
        basis_ref[1, :, F:],
        from_left.get((0,))[F : F + 4, :],
        from_left.get((1,))[F : F + 4, :],
        from_down_ref[F : F + 4, :],
    )
    for face in range(FACES):
        flat_ref[...] = jnp.zeros_like(flat_ref)
        for k, row in enumerate(face_slots(face)):
            flat_ref[row : row + 1, :] = sources[face][k : k + 1, :]
        high, middle, low = thirds(flat_ref[...])
        rows.held[face, 0:16, :] = high
        rows.held[face, 16:32, :] = middle
        rows.held[face, 32:48, :] = low
        parts = [p.astype(F32) for p in (high, high, high, middle, middle, low)]
        parts.append(jnp.zeros((32, F), F32))
        columns.held[face] = jnp.concatenate(parts, axis=0).T.astype(BF16)
    rows.send()
    columns.send()


def corner_onehot(numbers_t, axial, sector, spare):
    wanted = (axial & 15) * 32 + (sector & 31)
    columns = lax.broadcasted_iota(jnp.int32, (wanted.shape[0], CORNERS), 1)
    picks = jnp.where((columns == wanted) & jnp.logical_not(spare), 1.0, 0.0).astype(BF16)
    return nt(picks, numbers_t).astype(BF16)


def coarse_block_kernel(place_ref, numbers, inverse, first, later):
    blk, xh, near = place_ref[0], place_ref[1], place_ref[2]
    ids = lax.broadcasted_iota(jnp.int32, (CORNERS, CORNERS), 0)
    numbers_t = jnp.where(numbers.get()[...] == ids, 1.0, 0.0).astype(BF16)
    rows = lax.broadcasted_iota(jnp.int32, (16 * SLOTS, 1), 0)
    peer = rows >> 4
    entry = rows & 15
    third = (entry >= 3).astype(jnp.int32) + (entry >= 6).astype(jnp.int32) + (entry >= 9).astype(jnp.int32)
    da = third - 1
    ds = entry - 3 * third - 1
    spare = entry >= 12
    far_rows = corner_onehot(numbers_t, 2 * (peer >> 1) + da, (peer & 1) * 16 + near + ds, spare)
    near_rows = corner_onehot(numbers_t, 2 * blk + da, xh * 16 + peer + ds, spare)
    few = lax.broadcasted_iota(jnp.int32, (16 * 8, 1), 0)
    source, own = few >> 3, few & 7
    own_rows = corner_onehot(
        numbers_t, 2 * (source >> 1) + (own >> 1), (source & 1) * 16 + near + (own & 1), own >= 6
    )
    terms = thirds(inverse.get()[...])[::-1]
    picked = thirds(sum(nn(near_rows, part) for part in terms))[::-1]
    first.put(sum(nt(part, own_rows) for part in picked))
    block = sum(nt(part, far_rows) for part in picked).T
    columns = lax.broadcasted_iota(jnp.int32, (16 * SLOTS, 16 * SLOTS), 1) & 15
    passed = (columns == entry) & spare
    later.put(jnp.where(passed, 1.0, block))


HALVES = [((2, F, R), F32), ((2, F, R), F32), ((F, R), F32), ((F, R), F32), ((F, R), F32)]


def apply_block(s, operand_ref, left, right, up, down, mid, weights=None, seen=None):
    stores = {
        0: lambda v: right.put(v, (0,)),
        1: lambda v: right.put(v, (1,)),
        2: mid.put,
        3: up.put,
        4: lambda v: left.put(v, (0,)),
        5: lambda v: left.put(v, (1,)),
        6: down.put,
    }
    shared = None
    for k in range(2):
        for side in range(4):
            face = SIDES[k][side]
            image = nn(s.get(block_piece(k, side))[...], operand_ref[k])
            if face == 2:
                if shared is None:
                    shared = image
                    continue
                image = shared + image
            if weights is not None and face >= 4:
                image = image * weights[face - 4]
            stores[face](image)
            if seen is not None:
                seen(face, image)


def set_operand(operand_ref, face, value):
    value = value.astype(BF16)
    for k in range(2):
        for side in range(4):
            if SIDES[k][side] == face:
                operand_ref[k, side * F : (side + 1) * F, :] = value


def outer_weights(from_left, from_down):
    rows = [from_left.get((k,))[WEIGHT : WEIGHT + 1, :] for k in range(2)]
    rows.append(from_down.get()[WEIGHT : WEIGHT + 1, :])
    return [scale_column(row) for row in rows]


def first_kernel(r, from_left, from_down, s, left, right, up, down, mid, operand_ref):
    weights = outer_weights(from_left, from_down)
    set_operand(operand_ref, 6, from_down.get()[:F, :] * weights[2])
    for k in range(2):
        set_operand(operand_ref, 4 + k, from_left.get((k,))[:F, :] * weights[k])
    for face in range(4):
        set_operand(operand_ref, face, own_face(r, face))
    apply_block(s, operand_ref, left, right, up, down, mid, weights)


PLACES = ((1, (0,)), (1, (1,)), (4, ()), (2, ()), (0, (0,)), (0, (1,)), (3, ()))


def own_share(halves, face):
    which, piece = PLACES[face]
    return halves[which].get(piece)[...]


def assembled(halves, others, face):
    which, piece = PLACES[face]
    if which == 4:
        return own_share(halves, face)
    return own_share(halves, face) + others[which].get(piece)[...]


def stacked(values):
    high, middle, low = thirds(values)
    parts = [high, middle, low, high, middle, high, jnp.zeros((32, R), BF16)]
    return jnp.concatenate(parts, axis=0)


def face_loads(rows_ref, face, image):
    out = sum(nn(rows_ref[face], part) for part in thirds(image)[1::-1])
    return out[32:48] + out[16:32] + out[0:16]


def face_piece(face):
    return HALF_PIECES[(face % 2) * 2 + face // 2]


def own_face(r, face):
    return r.get(face_piece(face))[...]


def total(value):
    return jnp.sum(value, axis=0, keepdims=True)


def operate_first_kernel(
    values, columns, l0, r0, u0, d0, m0, fl, fr, fu, fd, r, rows, s,
    z, left, right, up, down, mid, message, corners_out, operand_ref, z_ref,
):
    corners = jnp.sum(values.get()[...], axis=0)
    corners_out.put(corners)
    terms = stacked(corners)
    columns_ref = columns.get()
    before, others = (l0, r0, u0, d0, m0), (fl, fr, fu, fd)
    images = (left, right, up, down, mid)
    progress = jnp.zeros((1, R), F32)
    for face in range(FACES):
        value = assembled(before, others, face) + nn(columns_ref[face], terms)
        z_ref[face] = value
        set_operand(operand_ref, face, value)
        if face < 4:
            z.put(value, (face,))
            progress = progress + total(own_face(r, face) * value)
    rows_ref = rows.get()
    sums = [jnp.zeros((SLOTS, R), F32), jnp.zeros((1, R), F32)]

    def seen(face, image):
        sums[0] = sums[0] + face_loads(rows_ref, face, image)
        sums[1] = sums[1] + total(z_ref[face] * image)

    apply_block(s, operand_ref, *images, seen=seen)
    loads, curvature = sums
    for peer in range(16):
        message.held[peer] = loads
        message.held[peer, 12:13, :] = progress
        message.held[peer, 13:14, :] = curvature
    message.send()


def second_kernel(
    values, corners_before, r_left, r_down, r, l0, r0, u0, d0, m0, fl, fr, fu, fd, s,
    residual, image_out, left, right, up, down, mid, corners_out, scalars, operand_ref,
):
    sums = jnp.sum(values.get()[...], axis=0)
    progress, curvature = sums[12:13, :], sums[13:14, :]
    alpha = progress / curvature
    corners_out.put(corners_before.get()[...] - alpha * sums)
    scalars.held[...] = jnp.zeros((8, R), F32)
    scalars.held[0:1, :] = progress
    scalars.held[1:2, :] = curvature
    scalars.held[2:3, :] = alpha
    scalars.send()
    before, others = (l0, r0, u0, d0, m0), (fl, fr, fu, fd)
    weights = outer_weights(r_left, r_down)
    for face in range(FACES):
        image = assembled(before, others, face)
        if face < 4:
            start = own_face(r, face)
        elif face < 6:
            start = r_left.get((face - 4,))[:F, :]
        else:
            start = r_down.get()[:F, :]
        value = start - alpha * image
        if face < 4:
            image_out.put(image, (face,))
            residual.put(value, (face,))
        else:
            value = value * weights[face - 4]
        set_operand(operand_ref, face, value)
    apply_block(s, operand_ref, left, right, up, down, mid, weights)


def operate_last_kernel(
    corners_in, columns, l0, r0, u0, d0, m0, fl, fr, fu, fd, residual, image_in, s,
    z, message, operand_ref, z_ref,
):
    corners = corners_in.get()[...]
    terms = stacked(jnp.where(lax.broadcasted_iota(jnp.int32, corners.shape, 0) < 12, corners, 0.0))
    columns_ref = columns.get()
    before, others = (l0, r0, u0, d0, m0), (fl, fr, fu, fd)
    progress = jnp.zeros((1, R), F32)
    mixed = jnp.zeros((1, R), F32)
    for face in range(FACES):
        value = assembled(before, others, face) + nn(columns_ref[face], terms)
        z_ref[face] = value
        set_operand(operand_ref, face, value)
        if face < 4:
            z.put(value, (face,))
            progress = progress + total(residual.get((face,))[...] * value)
            mixed = mixed + total(image_in.get((face,))[...] * value)
    curvature = jnp.zeros((1, R), F32)
    for k in range(2):
        for side in range(4):
            image = nn(s.get(block_piece(k, side))[...], operand_ref[k])
            face = SIDES[k][side]
            curvature = curvature + total(z_ref[face] * image)
    for peer in range(16):
        message.held[peer, 0:1, :] = progress
        message.held[peer, 1:2, :] = curvature
        message.held[peer, 2:3, :] = 2.0 * mixed
        message.held[peer, 3:4, :] = jnp.zeros((1, R), F32)
    message.send()


def finish_kernel(sums_in, scalars, z0, z1, out):
    sums = jnp.sum(sums_in.get()[...], axis=0)
    progress, curvature, mixed = sums[0:1, :], sums[1:2, :], sums[2:3, :]
    before = scalars.get()[...]
    first_progress, first_curvature, alpha = before[0:1, :], before[1:2, :], before[2:3, :]
    ratio = progress / first_progress
    last = progress / (curvature + ratio * (mixed + ratio * first_curvature))
    scale0 = alpha + last * ratio
    for face in (0, 2, 1, 3):
        out.put(scale0 * z0.get((face,))[...] + last * z1.get((face,))[...], face_piece(face))


def partial_kernel(message, block, out):
    flat = jnp.concatenate([message.get()[i] for i in range(16)], axis=0)
    values = jnp.dot(block.get()[...], flat, precision=EXACT, preferred_element_type=F32)
    for i in range(16):
        out.held[i] = values[i * SLOTS : (i + 1) * SLOTS]
    out.send()


def sum_kernel(near, out):
    sums = jnp.sum(near.get()[...], axis=0)
    for i in range(16):
        out.held[i] = sums
    out.send()


def moved(block, axes, count, distance):
    return lax.ppermute(block, axes, [(i, (i + distance) % count) for i in range(count)])


def exchanged(left, right, up, down):
    return (
        moved(right, CROSS, 32, 1),
        moved(left, CROSS, 32, -1),
        moved(down, BLK, 8, -1),
        moved(up, BLK, 8, 1),
    )


def on_device(r, s_inverse, s, basis, occ, left_order, down_order, numbers, coarse_inverse):
    r, s_inverse, s, basis = r[:, 0], s_inverse[:, 0], s[:, 0], basis[:, 0]
    place = jnp.stack([lax.axis_index(BLK), lax.axis_index("xh"), lax.axis_index(NEAR)]).astype(jnp.int32)
    operand = pltpu.VMEM((2, 4 * F, R), BF16)
    strip = pltpu.VMEM((F, 4 * F), BF16)

    right, up, loads = call(
        open_kernel, [((2, PACK, R), F32), ((PACK, R), F32), ((16, 8, R), F32)], r, occ, basis
    )
    r_left = moved(right, CROSS, 32, 1)
    r_down = moved(up, BLK, 8, 1)
    far = lax.all_to_all(loads, FAR, 0, 0)
    first_block, later_block = call(
        coarse_block_kernel,
        [((16 * SLOTS, 16 * 8), F32), ((16 * SLOTS, 16 * SLOTS), F32)],
        place, numbers[None, :], coarse_inverse,
        smem=(0,), near_out=(0, 1),
    )
    schur_block, schur_here = call(
        reorder_weighted_kernel,
        [(s.shape, BF16), (s.shape, BF16)],
        s, left_order, down_order, occ,
        near_out=(1,), scratch=[strip],
    )
    r_left, r_down, first_block, later_block, schur_here = lax.optimization_barrier(
        (r_left, r_down, first_block, later_block, schur_here)
    )

    halves = call(
        first_kernel, HALVES, r, r_left, r_down, schur_here,
        near=(1, 2, 3), scratch=[operand],
    )
    far, s_inverse, *halves = lax.optimization_barrier((far, s_inverse, *halves))
    others = exchanged(*halves[:4])
    (partial,) = call(partial_kernel, [((16, SLOTS, R), F32)], far, first_block, near=(0, 1))
    values = lax.all_to_all(partial, NEAR, 0, 0)
    (inverse_block,) = call(
        reorder_plain_kernel,
        [(s_inverse.shape, BF16)],
        s_inverse, left_order, down_order,
        scratch=[strip],
    )
    rows, columns = call(
        basis_kernel,
        [((FACES, 48, F), BF16), ((FACES, F, 128), BF16)],
        basis, r_left, r_down,
        scratch=[pltpu.VMEM((SLOTS, F), F32)],
    )
    z0, *halves, message, corners = call(
        operate_first_kernel,
        [((4, F, R), F32), *HALVES, ((16, SLOTS, R), F32), ((SLOTS, R), F32)],
        values, columns, *halves, *others, r, rows, inverse_block,
        near=(0, 7, 8, 9, 10), scratch=[operand, pltpu.VMEM((FACES, F, R), F32)],
    )
    others = exchanged(*halves[:4])
    near = lax.all_to_all(message, NEAR, 0, 0)
    (partial,) = call(partial_kernel, [((16, SLOTS, R), F32)], near, later_block, near=(0, 1))
    values = lax.all_to_all(partial, FAR, 0, 0)
    residual, image, *halves, corners, scalars = call(
        second_kernel,
        [((4, F, R), F32), ((4, F, R), F32), *HALVES, ((SLOTS, R), F32), ((8, R), F32)],
        values, corners, r_left, r_down, r, *halves, *others, schur_block,
        near=(0, 10, 11, 12, 13), near_out=(0, 1, 2, 3, 4, 5, 6, 7), scratch=[operand],
    )
    others = exchanged(*halves[:4])
    z1, message = call(
        operate_last_kernel,
        [((4, F, R), F32), ((16, 4, R), F32)],
        corners, columns, *halves, *others, residual, image, inverse_block,
        near=tuple(range(14)), near_out=(0,), scratch=[operand, pltpu.VMEM((FACES, F, R), F32)],
    )
    near = lax.all_to_all(message, NEAR, 0, 0)
    (spread_sums,) = call(sum_kernel, [((16, 4, R), F32)], near, near=(0,))
    sums = lax.all_to_all(spread_sums, FAR, 0, 0)
    (out,) = call(finish_kernel, [((2, 2 * F, R), F32)], sums, scalars, z0, z1, near=(0, 1, 2, 3))
    return out[:, None]


def solution(mesh):
    split = Mesh(mesh.devices.reshape(tuple(SPLIT.values())), tuple(SPLIT))
    four = P(BLK, CROSS, None, None)
    three = P(BLK, CROSS, None)
    return jax.shard_map(
        on_device,
        mesh=split,
        in_specs=(four, four, four, four, three, three, three, P(), P()),
        out_specs=four,
        check_vma=False,
    )
```
